128 devices in a mesh: expert: 32 (over y, x, core), blk: 4 (over z).
Axes of the slice: x: 4, y: 4, z: 4, core: 2. Of those that a mesh axis runs over, the one named last changes fastest.
Arguments:
- tokens: bfloat16 [8192, 7168], P(('expert', 'blk')), may hold values from -6 to 6
- route_ids: int32 [8192, 8], P(('expert', 'blk')), may hold values from 0 to 31, all different within a row; in each aligned block of 64 rows (0 to 63, 64 to 127, ...) at most 20 rows name the same one
- route_gates: float32 [8192, 8], P(('expert', 'blk')), may hold values from 0.2 to 1
- gate_weight: bfloat16 [32, 1024, 7168], P('expert', 'blk'), may hold values from -0.0625 to 0.0625
- up_weight: bfloat16 [32, 1024, 7168], P('expert', 'blk'), may hold values from -0.0625 to 0.0625
- down_weight: bfloat16 [32, 1024, 7168], P('expert', 'blk'), may hold values from -0.1875 to 0.1875
Outputs:
- mixed: bfloat16 [8192, 7168], P(('expert', 'blk'))
The draws below stay inside these ranges and needn't reach their ends.
Inputs may be any that keep to these rules, and one draw needn't show every extreme that they name: `route_ids`: each row names 8 different experts. Within the 64 rows of one device no expert is named by more than 20 rows, a bound that some block reaches.
All inputs are finite; a program needn't handle non-finite values.
Results may differ from the reference program's by a relative error of at most 0.011.
Values may be sent and summed in bfloat16 or wider, within the bound.
No kernel may reach another device: no remote copies, remote signals or barrier semaphores. Data moves between devices by JAX's collectives and lax.ppermute only.
A program may use at most 256 MiB of HBM per device.

```python
import math
import jax
import jax.numpy as jnp
import numpy as np
from jax import lax

D = 7168
FFW = 1024
TOP = 8
TOK_DEV = 64
EXPERTS = 32
TOKENS = 8192
CAP = 20


def levels(rng, dims, pieces, low, largest):
    loudness = 1.0
    for dim, blocks in pieces:
        steps = jax.random.uniform(jax.random.fold_in(jax.random.fold_in(rng, 6), dim), (blocks,), jnp.float32, low / len(pieces), largest / len(pieces))
        loudness = loudness * jnp.repeat(jnp.exp(steps), dims[dim] // blocks).reshape((-1,) + (1,) * (len(dims) - 1 - dim))
    return loudness


def assign_block(own_key, own, number, rows, number_of, top, most, slope):
    order = jax.random.permutation(own_key, number_of)
    heavy_load, common = load_shares(number_of, rows * top, most, slope, True), load_shares(number_of, rows * top, most, slope, False)
    places = jnp.arange(number_of)

    def named(lengths, offset_by):
        used = int((lengths > 0).sum())
        fixed = max(1, used // 4)
        shifted = fixed + (places - fixed + offset_by * (used - fixed)) % max(1, number_of - fixed)
        return jnp.zeros((number_of,), jnp.int32).at[order[jnp.where(places < fixed, places, shifted)]].set(jnp.asarray(lengths, jnp.int32))

    lengths = jnp.where(number % 4 == 0, named(heavy_load, number // 4), named(common, number - number // 4 - 1))
    mixed = jax.random.permutation(jax.random.fold_in(own, 3), number_of)
    source_of, sink = mixed[0:number_of // 2 * 2:2], mixed[1:number_of // 2 * 2:2]
    margin = jnp.minimum(lengths[source_of] - 1, most - lengths[sink]) // 2
    margin = jnp.where((source_of == order[0]) | (sink == order[0]) | (lengths[sink] == 0), 0, jnp.maximum(margin, 0))
    shifted = jax.random.randint(jax.random.fold_in(own, 4), (number_of // 2,), 0, 1 << 20) % (margin + 1)
    lengths = lengths.at[source_of].add(-shifted).at[sink].add(shifted)
    labels = jnp.searchsorted(jnp.cumsum(lengths), jnp.arange(rows * top), side="right").astype(jnp.int32)
    grid = labels.reshape(top, rows).T
    grid = grid[jax.random.permutation(jax.random.fold_in(own, 1), rows)]
    offset_by = jax.random.randint(jax.random.fold_in(own, 2), (rows, 1), 0, top)
    return jnp.take_along_axis(grid, (jnp.arange(top)[None, :] + offset_by) % top, axis=1)


def load_shares(amount, total, limit, slope, full):
    portions = [(1 << 20) // math.isqrt(rank ** slope) + 1 for rank in range(1, amount + 1)]
    largest = limit if full else min(limit, max(-(-total // amount), total * portions[0] // sum(portions)))
    least = 1 if total - largest >= amount - 1 else 0
    given, rest = [largest] + [least] * (amount - 1), total - largest - least * (amount - 1)
    while rest > 0:
        candidates = [i for i in range(1, amount) if given[i] < largest] or [i for i in range(1, amount) if given[i] < limit]
        whole, budget = sum([portions[i] for i in candidates]), rest
        for i in candidates:
            extra = min(limit - given[i], max(1, budget * portions[i] // whole), rest)
            given[i] = given[i] + extra
            rest = rest - extra
    return np.array(given)


def bell_draw(key, dims, spread, bound, pieces=(), kind=jnp.bfloat16):
    gain = levels(key, dims, pieces, -0.22, 0.18) if pieces else 1.0
    array = jax.random.normal(key, dims, jnp.float32) * spread * gain
    return jnp.minimum(jnp.maximum(array, -bound), bound).astype(kind)


def setup_inputs(seed: int = 0) -> dict:
    key_list = jax.random.split(jax.random.key(seed), 7)
    tokens = bell_draw(key_list[0], (TOKENS, D), 1.0, 6.0, ((0, 128),))
    route_ids_keys = jax.random.split(jax.random.fold_in(key_list[1], 1), TOKENS // TOK_DEV)
    route_ids_turns = jax.random.permutation(jax.random.fold_in(key_list[1], 3), TOKENS // TOK_DEV)
    route_ids = jax.vmap(lambda own, number: assign_block(jax.random.fold_in(key_list[1], 2), own, number, TOK_DEV, EXPERTS, TOP, CAP, 2))(route_ids_keys, route_ids_turns).reshape((TOKENS, TOP))
    route_gates = jnp.clip(0.2 + 0.8 * jax.random.uniform(key_list[2], (TOKENS, TOP), jnp.float32) ** levels(key_list[2], (TOKENS, TOP), ((0, 128),), -0.2, 0.2), 0.2, 1.0)
    gate_weight = bell_draw(key_list[3], (EXPERTS, FFW, D), D ** -0.5, 0.0625, ((0, 32), (1, 4)))
    up_weight = bell_draw(key_list[4], (EXPERTS, FFW, D), D ** -0.5, 0.0625, ((0, 32), (1, 4)))
    down_weight = bell_draw(key_list[5], (EXPERTS, FFW, D), FFW ** -0.5, 0.1875, ((0, 32), (1, 4)))
    return {"tokens": tokens, "route_ids": route_ids, "route_gates": route_gates, "gate_weight": gate_weight, "up_weight": up_weight, "down_weight": down_weight}


def reference(tokens, route_ids, route_gates, gate_weight, up_weight, down_weight):
    flat_ids = route_ids.reshape(-1).astype(jnp.int32)
    flat_gate = route_gates.reshape(-1).astype(jnp.float32)
    flat_tok = (jnp.arange(TOKENS * TOP) // TOP).astype(jnp.int32)
    most_rows = (TOKENS // TOK_DEV) * CAP
    block_rows = math.gcd(128, most_rows)
    block_count = most_rows // block_rows

    def per_expert(expert, total):
        match = flat_ids == expert
        place = (jnp.cumsum(match.astype(jnp.int32)) - 1).astype(jnp.int32)
        target = jnp.where(match, place, most_rows).astype(jnp.int32)
        row_index = jnp.zeros((most_rows,), jnp.int32).at[target].set(flat_tok, mode="drop")
        row_weight = jnp.zeros((most_rows,), jnp.float32).at[target].set(flat_gate, mode="drop")
        count = jnp.sum(match.astype(jnp.int32)).astype(jnp.int32)
        w_gate = gate_weight[expert]
        w_up = up_weight[expert]
        w_down = down_weight[expert]

        def one_block(block, acc):
            start = (block * block_rows).astype(jnp.int32)

            def compute(inner):
                index = lax.dynamic_slice_in_dim(row_index, start, block_rows, 0)
                weight = lax.dynamic_slice_in_dim(row_weight, start, block_rows, 0)
                rows = tokens[index]
                gate = lax.dot_general(rows, w_gate, (((1,), (1,)), ((), ())), preferred_element_type=jnp.float32)
                upper = lax.dot_general(rows, w_up, (((1,), (1,)), ((), ())), preferred_element_type=jnp.float32)
                hidden = (jax.nn.silu(gate) * upper).astype(jnp.bfloat16)
                result = jnp.dot(hidden, w_down, preferred_element_type=jnp.float32).astype(jnp.bfloat16)
                return inner.at[index].add(result.astype(jnp.float32) * weight[:, None])

            return lax.cond(start < count, compute, lambda inner: inner, acc)

        return lax.fori_loop(0, block_count, one_block, total)

    total = jnp.zeros((TOKENS, D), jnp.float32)
    total = lax.fori_loop(0, EXPERTS, per_expert, total)
    return total.astype(jnp.bfloat16)
```

```python
import jax
import jax.numpy as jnp
from jax import lax
from jax.sharding import Mesh, PartitionSpec as P

EXP = ("y", "x", "c")
COL = ("c", "zh", "zl")
ALL = ("y", "x", "c", "zh", "zl")


def swaps(*pairs):
    return [way for a, b in pairs for way in ((a, b), (b, a))]


PAIR = swaps((0, 3), (1, 2))
NEXT = swaps((0, 1), (6, 7), (4, 3), (5, 2))
FAR = swaps((5, 3), (4, 2))
SIBLING = swaps((0, 4), (1, 5), (2, 6), (3, 7))
FROM_HOME = [(0, 4), (1, 5), (6, 2), (7, 3)]
TO_HOME = [(b, a) for a, b in FROM_HOME]
CHUNKS = 4


def along(value, pairs):
    return lax.ppermute(value, COL, pairs)


def spread(own, home):
    near = along(own, NEXT)
    far = along(own, FAR)
    return (
        jnp.where(home, own, along(own, FROM_HOME)),
        near,
        along(near, SIBLING),
        jnp.where(home, along(far, TO_HOME), far),
    )


def hidden_units(rows, panel_gate, panel_up):
    gate = lax.dot_general(
        rows, panel_gate, (((1,), (1,)), ((), ())), preferred_element_type=jnp.float32
    )
    upper = lax.dot_general(
        rows, panel_up, (((1,), (1,)), ((), ())), preferred_element_type=jnp.float32
    )
    return (jax.nn.silu(gate) * upper).astype(jnp.bfloat16)


def pair_exchange(value):
    return lax.ppermute(value, ("zh", "zl"), PAIR)


def body(tokens, route_ids, route_gates, gate_weight, up_weight, down_weight):
    tok_rows, width = tokens.shape
    chips = lax.axis_size("y") * lax.axis_size("x")
    side = lax.axis_index("zh")
    home = lax.axis_index("c") == side

    other = pair_exchange(tokens)
    routes = jnp.concatenate([route_ids.astype(jnp.float32), route_gates], axis=1)
    routes = jnp.concatenate([routes, pair_exchange(routes)], axis=0)
    both = jnp.concatenate([tokens, other], axis=0)

    gates = spread(gate_weight[0], home)
    uppers = spread(up_weight[0], home)
    step = width // CHUNKS
    downs = [spread(down_weight[0][:, j * step : (j + 1) * step], home) for j in range(CHUNKS)]

    top = route_ids.shape[1]
    hosted = (2 * jnp.arange(chips, dtype=jnp.int32) + side).astype(jnp.float32)
    match = (routes[:, :top, None] == hosted[None, None, :]).astype(jnp.float32)
    named = jnp.sum(match, axis=1)
    weight = jnp.sum(routes[:, top:, None] * match, axis=1)
    count = 2 * tok_rows
    earlier = (jnp.arange(count)[:, None] > jnp.arange(count)[None, :]).astype(jnp.bfloat16)
    rank = jnp.dot(earlier, named.astype(jnp.bfloat16), preferred_element_type=jnp.float32)
    on_slot = (rank[:, :, None] == jnp.arange(40, dtype=jnp.float32)) & (named[:, :, None] > 0)
    pick = jnp.transpose(on_slot, (1, 2, 0)).astype(jnp.bfloat16)
    mix = jnp.where(on_slot, weight[:, :, None], 0.0)

    def rows_of(part):
        flat = part.reshape(-1, count)
        return jnp.dot(flat, both, preferred_element_type=jnp.float32).astype(jnp.bfloat16)

    def halves(part):
        part = part.reshape(count, -1)
        high = lax.reduce_precision(part, 8, 7)
        return jnp.concatenate([high, part - high], axis=0).astype(jnp.bfloat16)

    mix_main, mix_rest = halves(mix[:, :, :32]), halves(mix[:, :, 32:])

    def exchange(main, rest, columns):
        got = lax.all_to_all(main.reshape(2 * chips, 16, columns), EXP, 0, 0, tiled=True)
        got_rest = lax.all_to_all(rest.reshape(chips, 8, columns), ("y", "x"), 0, 0, tiled=True)
        return got.reshape(-1, columns), got_rest.reshape(-1, columns)

    main, rest = exchange(rows_of(pick[:, :32]), rows_of(pick[:, 32:]), width)
    rows = jnp.concatenate([main, rest], axis=0)
    hidden = jnp.concatenate(
        [hidden_units(rows, g, u) for g, u in zip(gates, uppers, strict=True)], axis=1
    )
    outs = []
    for j in range(CHUNKS):
        result = jnp.dot(
            hidden, jnp.concatenate(downs[j], axis=0), preferred_element_type=jnp.float32
        ).astype(jnp.bfloat16)
        back, back_rest = exchange(result[:512], result[512:], step)
        sums = jnp.dot(mix_main, back, preferred_element_type=jnp.float32) + jnp.dot(
            mix_rest, back_rest, preferred_element_type=jnp.float32
        )
        sums = sums[:count] + sums[count:]
        share = pair_exchange(sums[tok_rows:].astype(jnp.bfloat16))
        outs.append((sums[:tok_rows] + share.astype(jnp.float32)).astype(jnp.bfloat16))
    return jnp.concatenate(outs, axis=1)


def solution(mesh):
    fine = Mesh(mesh.devices.reshape(4, 4, 2, 2, 2), ALL)
    rows = P(ALL, None)
    panels = P(EXP, ("zh", "zl"), None)
    return jax.shard_map(
        body,
        mesh=fine,
        in_specs=(rows, rows, rows, panels, panels, panels),
        out_specs=rows,
        check_vma=False,
    )
```

```python
import functools

import jax
import jax.numpy as jnp
from jax import lax
from jax.experimental import pallas as pl
from jax.experimental.pallas import tpu as pltpu
from jax.sharding import Mesh, PartitionSpec as P

EXP = ("y", "x", "c")
COL = ("c", "zh", "zl")
ALL = ("y", "x", "c", "zh", "zl")


def swaps(*pairs):
    return [way for a, b in pairs for way in ((a, b), (b, a))]


PAIR = swaps((0, 3), (1, 2))
NEXT = swaps((0, 1), (6, 7), (4, 3), (5, 2))
FAR = swaps((5, 3), (4, 2))
SIBLING = swaps((0, 4), (1, 5), (2, 6), (3, 7))
FROM_HOME = [(0, 4), (1, 5), (6, 2), (7, 3)]
TO_HOME = [(b, a) for a, b in FROM_HOME]
STEPS = (1792, 2688, 2688)
QUARTER = 256
MAIN = 512
REST = 128
TILE = 896
DEEP = 1792


def along(value, pairs):
    return lax.ppermute(value, COL, pairs)


def after(value, *earlier):
    return lax.optimization_barrier((value, *earlier))[0]


def spread(own, before):
    near_before, far_before = before
    near = along(after(own, *near_before), NEXT)
    far = along(after(own, *far_before), FAR)
    panels = (own, along(own, FROM_HOME), near, along(near, SIBLING), along(far, TO_HOME), far)
    return panels, ((near,), (far,))


def pick_block(flag, wanted, block):
    return jnp.where(flag[0] == wanted, block, 0)


def hidden_kernel(flag, *refs, quarters):
    main, rest = refs[:2]
    panels, out, gate_sum, up_sum = refs[2:-3], refs[-3], refs[-2], refs[-1]
    part = pl.program_id(0)

    @pl.when(part == 0)
    def _():
        gate_sum[...] = jnp.zeros_like(gate_sum)
        up_sum[...] = jnp.zeros_like(up_sum)

    def add(total, place, weights):
        for rows, first, number in ((main, 0, MAIN), (rest, MAIN, REST)):
            total[pl.ds(first, number), pl.ds(place * QUARTER, QUARTER)] += lax.dot_general(
                rows[...], weights, (((1,), (1,)), ((), ())), preferred_element_type=jnp.float32
            )

    at = 0
    for place, kind in enumerate(quarters):
        if kind == 1:
            gate, upper = panels[at][...], panels[at + 1][...]
        else:
            home = flag[0] == 1
            gate = jnp.where(home, panels[at][...], panels[at + 2][...])
            upper = jnp.where(home, panels[at + 1][...], panels[at + 3][...])
        add(gate_sum, place, gate)
        add(up_sum, place, upper)
        at += 2 * kind

    @pl.when(part == pl.num_programs(0) - 1)
    def _():
        gate = gate_sum[...]
        out[...] = (gate / (1.0 + jnp.exp(-gate)) * up_sum[...]).astype(out.dtype)


def hidden_units(flag, main, rest, quarters):
    width = main.shape[1]
    count = len(quarters)
    kinds = tuple(len(quarter) for quarter in quarters)
    specs = [
        pl.BlockSpec((MAIN, DEEP), lambda i, f: (0, i)),
        pl.BlockSpec((REST, DEEP), lambda i, f: (0, i)),
    ]
    operands = [main, rest]
    for quarter in quarters:
        for place, (gate, upper) in enumerate(quarter):
            if len(quarter) == 1:
                spec = pl.BlockSpec((QUARTER, DEEP), lambda i, f: (0, i))
            else:
                spec = pl.BlockSpec(
                    (QUARTER, DEEP), lambda i, f, w=1 - place: (0, pick_block(f, w, i))
                )
            specs += [spec, spec]
            operands += [gate, upper]
    rows = MAIN + REST
    return pl.pallas_call(
        functools.partial(hidden_kernel, quarters=kinds),
        grid_spec=pltpu.PrefetchScalarGridSpec(
            num_scalar_prefetch=1,
            grid=(width // DEEP,),
            in_specs=specs,
            out_specs=pl.BlockSpec((rows, count * QUARTER), lambda i, f: (0, 0)),
            scratch_shapes=[pltpu.VMEM((rows, count * QUARTER), jnp.float32)] * 2,
        ),
        out_shape=jax.ShapeDtypeStruct((rows, count * QUARTER), jnp.bfloat16),
        compiler_params=pltpu.CompilerParams(vmem_limit_bytes=48 * 2**20),
        cost_estimate=pl.CostEstimate(
            flops=4 * rows * width * count * QUARTER,
            bytes_accessed=2 * width * (rows + 2 * count * QUARTER),
            transcendentals=rows * count * QUARTER,
        ),
    )(flag, *operands)


def down_kernel(flag, first, last, own, copied, near, across, brought, far, out_main, out_rest):
    home = flag[0] == 1
    panels = (
        (first[:, :QUARTER], jnp.where(home, own[...], copied[...])),
        (first[:, QUARTER : 2 * QUARTER], near[...]),
        (first[:, 2 * QUARTER :], across[...]),
        (last[...], jnp.where(home, brought[...], far[...])),
    )
    total = None
    for hidden, weights in panels:
        term = jnp.dot(hidden, weights, preferred_element_type=jnp.float32)
        total = term if total is None else total + term
    total = total.astype(out_main.dtype)
    out_main[...] = total[:MAIN]
    out_rest[...] = total[MAIN:]


def down_rows(flag, first, last, panels):
    step = panels[0].shape[1]
    rows = MAIN + REST

    def panel(wanted=None):
        if wanted is None:
            return pl.BlockSpec((QUARTER, TILE), lambda i, f: (0, i))
        return pl.BlockSpec((QUARTER, TILE), lambda i, f: (0, pick_block(f, wanted, i)))

    return pl.pallas_call(
        down_kernel,
        grid_spec=pltpu.PrefetchScalarGridSpec(
            num_scalar_prefetch=1,
            grid=(step // TILE,),
            in_specs=[
                pl.BlockSpec(first.shape, lambda i, f: (0, 0)),
                pl.BlockSpec(last.shape, lambda i, f: (0, 0)),
                panel(1),
                panel(0),
                panel(),
                panel(),
                panel(1),
                panel(0),
            ],
            out_specs=[
                pl.BlockSpec((MAIN, TILE), lambda i, f: (0, i)),
                pl.BlockSpec((REST, TILE), lambda i, f: (0, i)),
            ],
        ),
        out_shape=[
            jax.ShapeDtypeStruct((MAIN, step), jnp.bfloat16),
            jax.ShapeDtypeStruct((REST, step), jnp.bfloat16),
        ],
        compiler_params=pltpu.CompilerParams(vmem_limit_bytes=32 * 2**20),
        cost_estimate=pl.CostEstimate(
            flops=8 * rows * QUARTER * step,
            bytes_accessed=2 * (4 * QUARTER * step + rows * (4 * QUARTER + step)),
            transcendentals=0,
        ),
    )(flag, first, last, *panels)


def pair_exchange(value):
    return lax.ppermute(value, ("zh", "zl"), PAIR)


def body(tokens, route_ids, route_gates, gate_weight, up_weight, down_weight):
    tok_rows, width = tokens.shape
    chips = lax.axis_size("y") * lax.axis_size("x")
    side = lax.axis_index("zh")
    flag = (lax.axis_index("c") == side).astype(jnp.int32).reshape(1)

    routes = jnp.concatenate([route_ids.astype(jnp.float32), route_gates], axis=1)
    routes = jnp.concatenate([routes, pair_exchange(routes)], axis=0)
    both = jnp.concatenate([tokens, pair_exchange(tokens)], axis=0)

    gates, order = spread(gate_weight[0], ((), ()))
    uppers, order = spread(up_weight[0], order)
    downs, at = [], 0
    for step in STEPS:
        panels, order = spread(down_weight[0][:, at : at + step], order)
        downs.append(panels)
        at += step

    top = route_ids.shape[1]
    hosted = (2 * jnp.arange(chips, dtype=jnp.int32) + side).astype(jnp.float32)
    match = (routes[:, :top, None] == hosted[None, None, :]).astype(jnp.float32)
    named = jnp.sum(match, axis=1)
    weight = jnp.sum(routes[:, top:, None] * match, axis=1)
    count = 2 * tok_rows
    place = jnp.arange(count)
    earlier = (place[:, None] > place[None, :]).astype(jnp.bfloat16)
    rank = jnp.dot(earlier, named.astype(jnp.bfloat16), preferred_element_type=jnp.float32)
    on_slot = (rank[:, :, None] == jnp.arange(40, dtype=jnp.float32)) & (named[:, :, None] > 0)
    pick = jnp.transpose(on_slot, (1, 2, 0)).astype(jnp.bfloat16)
    mix = jnp.where(on_slot, weight[:, :, None], 0.0)

    def rows_of(part):
        flat = part.reshape(-1, count)
        return jnp.dot(flat, both, preferred_element_type=jnp.float32).astype(jnp.bfloat16)

    def halves(part):
        part = part.reshape(count, -1)
        high = lax.reduce_precision(part, 8, 7)
        return jnp.concatenate([high, part - high], axis=0).astype(jnp.bfloat16)

    mix_main, mix_rest = halves(mix[:, :, :32]), halves(mix[:, :, 32:])

    def exchange(main, rest):
        columns = main.shape[-1]
        got = lax.all_to_all(main.reshape(2 * chips, 16, columns), EXP, 0, 0, tiled=True)
        got_rest = lax.all_to_all(rest.reshape(chips, 8, columns), ("y", "x"), 0, 0, tiled=True)
        return got.reshape(-1, columns), got_rest.reshape(-1, columns)

    main, rest = exchange(rows_of(pick[:, :32]), rows_of(pick[:, 32:]))
    pairs = list(zip(gates, uppers, strict=True))
    first = hidden_units(flag, main, rest, [pairs[:2], pairs[2:3], pairs[3:4]])
    last = hidden_units(flag, main, rest, [pairs[4:]])
    outs = []
    for panels in downs:
        back, back_rest = exchange(*down_rows(flag, first, last, panels))
        sums = jnp.dot(mix_main, back, preferred_element_type=jnp.float32) + jnp.dot(
            mix_rest, back_rest, preferred_element_type=jnp.float32
        )
        sums = sums[:count] + sums[count:]
        share = pair_exchange(sums[tok_rows:].astype(jnp.bfloat16))
        outs.append((sums[:tok_rows] + share.astype(jnp.float32)).astype(jnp.bfloat16))
    return jnp.concatenate(outs, axis=1)


def solution(mesh):
    fine = Mesh(mesh.devices.reshape(4, 4, 2, 2, 2), ALL)
    rows = P(ALL, None)
    panels = P(EXP, ("zh", "zl"), None)
    return jax.shard_map(
        body,
        mesh=fine,
        in_specs=(rows, rows, rows, panels, panels, panels),
        out_specs=rows,
        check_vma=False,
    )
```

```python
import functools

import jax
import jax.numpy as jnp
from jax import lax
from jax.experimental import pallas as pl
from jax.experimental.pallas import tpu as pltpu
from jax.sharding import Mesh, PartitionSpec as P

EXP = ("y", "x", "c")
COL = ("c", "zh", "zl")
ALL = ("y", "x", "c", "zh", "zl")


def swaps(*pairs):
    return [way for a, b in pairs for way in ((a, b), (b, a))]


PAIR = swaps((0, 3), (1, 2))
NEXT = swaps((0, 1), (6, 7), (4, 3), (5, 2))
FAR = swaps((5, 3), (4, 2))
SIBLING = swaps((0, 4), (1, 5), (2, 6), (3, 7))
FROM_HOME = [(0, 4), (1, 5), (6, 2), (7, 3)]
TO_HOME = [(b, a) for a, b in FROM_HOME]
STEPS = (1792, 2688, 2688)
QUARTER = 256
MAIN = 256
REST = 128
TILE = 896
DEEP = 1792


def along(value, pairs):
    return lax.ppermute(value, COL, pairs)


def after(value, *earlier):
    return lax.optimization_barrier((value, *earlier))[0]


def share(own, near, far, near_after, far_after):
    across = along(after(near, near_after), SIBLING)
    brought = along(after(far, far_after), TO_HOME)
    return own, along(own, FROM_HOME), near, across, brought, far


def pick_block(flag, wanted, block):
    return jnp.where(flag[0] == wanted, block, 0)


def hidden_kernel(flag, *refs, quarters):
    mine, theirs, rest = refs[:3]
    panels, out, gate_sum, up_sum = refs[3:-3], refs[-3], refs[-2], refs[-1]
    part = pl.program_id(0)

    @pl.when(part == 0)
    def _():
        gate_sum[...] = jnp.zeros_like(gate_sum)
        up_sum[...] = jnp.zeros_like(up_sum)

    def add(total, place, weights):
        for rows, first in ((mine, 0), (theirs, MAIN), (rest, 2 * MAIN)):
            number = rows.shape[0]
            total[pl.ds(first, number), pl.ds(place * QUARTER, QUARTER)] += lax.dot_general(
                rows[...], weights, (((1,), (1,)), ((), ())), preferred_element_type=jnp.float32
            )

    at = 0
    for place, kind in enumerate(quarters):
        if kind == 1:
            both = panels[at][...]
        else:
            both = jnp.where(flag[0] == 1, panels[at][...], panels[at + 1][...])
        add(gate_sum, place, both[:QUARTER])
        add(up_sum, place, both[QUARTER:])
        at += kind

    @pl.when(part == pl.num_programs(0) - 1)
    def _():
        gate = gate_sum[...]
        out[...] = (gate / (1.0 + jnp.exp(-gate)) * up_sum[...]).astype(out.dtype)


def hidden_units(flag, mine, theirs, rest, quarters):
    width = rest.shape[1]
    count = len(quarters)
    kinds = tuple(len(quarter) for quarter in quarters)
    specs = [
        pl.BlockSpec((MAIN, DEEP), lambda i, f: (0, i)),
        pl.BlockSpec((MAIN, DEEP), lambda i, f: (0, i)),
        pl.BlockSpec((REST, DEEP), lambda i, f: (0, i)),
    ]
    operands = [mine, theirs, rest]
    for quarter in quarters:
        for place, both in enumerate(quarter):
            if len(quarter) == 1:
                spec = pl.BlockSpec((2 * QUARTER, DEEP), lambda i, f: (0, i))
            else:
                spec = pl.BlockSpec(
                    (2 * QUARTER, DEEP), lambda i, f, w=1 - place: (0, pick_block(f, w, i))
                )
            specs.append(spec)
            operands.append(both)
    rows = 2 * MAIN + REST
    return pl.pallas_call(
        functools.partial(hidden_kernel, quarters=kinds),
        grid_spec=pltpu.PrefetchScalarGridSpec(
            num_scalar_prefetch=1,
            grid=(width // DEEP,),
            in_specs=specs,
            out_specs=pl.BlockSpec((rows, count * QUARTER), lambda i, f: (0, 0)),
            scratch_shapes=[pltpu.VMEM((rows, count * QUARTER), jnp.float32)] * 2,
        ),
        out_shape=jax.ShapeDtypeStruct((rows, count * QUARTER), jnp.bfloat16),
        compiler_params=pltpu.CompilerParams(vmem_limit_bytes=48 * 2**20),
        cost_estimate=pl.CostEstimate(
            flops=4 * rows * width * count * QUARTER,
            bytes_accessed=2 * width * (rows + 2 * count * QUARTER),
            transcendentals=rows * count * QUARTER,
        ),
    )(flag, *operands)


def down_kernel(flag, first, last, own, copied, near, across, brought, far, out_main, out_rest):
    home = flag[0] == 1
    panels = (
        (first[:, :QUARTER], jnp.where(home, own[...], copied[...])),
        (first[:, QUARTER : 2 * QUARTER], near[...]),
        (first[:, 2 * QUARTER :], across[...]),
        (last[...], jnp.where(home, brought[...], far[...])),
    )
    total = None
    for hidden, weights in panels:
        term = jnp.dot(hidden, weights, preferred_element_type=jnp.float32)
        total = term if total is None else total + term
    total = total.astype(out_main.dtype)
    out_main[:, :8] = total[:MAIN].reshape(-1, 8, TILE)
    out_main[:, 8:] = total[MAIN : 2 * MAIN].reshape(-1, 8, TILE)
    out_rest[...] = total[2 * MAIN :]


def down_rows(flag, first, last, panels):
    step = panels[0].shape[1]
    rows = 2 * MAIN + REST

    def panel(wanted=None):
        if wanted is None:
            return pl.BlockSpec((QUARTER, TILE), lambda i, f: (0, i))
        return pl.BlockSpec((QUARTER, TILE), lambda i, f: (0, pick_block(f, wanted, i)))

    main, tail = pl.pallas_call(
        down_kernel,
        grid_spec=pltpu.PrefetchScalarGridSpec(
            num_scalar_prefetch=1,
            grid=(step // TILE,),
            in_specs=[
                pl.BlockSpec(first.shape, lambda i, f: (0, 0)),
                pl.BlockSpec(last.shape, lambda i, f: (0, 0)),
                panel(1),
                panel(0),
                panel(),
                panel(),
                panel(1),
                panel(0),
            ],
            out_specs=[
                pl.BlockSpec((MAIN // 8, 16, TILE), lambda i, f: (0, 0, i)),
                pl.BlockSpec((REST, TILE), lambda i, f: (0, i)),
            ],
        ),
        out_shape=[
            jax.ShapeDtypeStruct((MAIN // 8, 16, step), jnp.bfloat16),
            jax.ShapeDtypeStruct((REST, step), jnp.bfloat16),
        ],
        compiler_params=pltpu.CompilerParams(vmem_limit_bytes=32 * 2**20),
        cost_estimate=pl.CostEstimate(
            flops=8 * rows * QUARTER * step,
            bytes_accessed=2 * (4 * QUARTER * step + rows * (4 * QUARTER + step)),
            transcendentals=0,
        ),
    )(flag, first, last, *panels)
    return main.reshape(2 * MAIN, step), tail


def pair_exchange(value):
    return lax.ppermute(value, ("zh", "zl"), PAIR)


def body(tokens, route_ids, route_gates, gate_weight, up_weight, down_weight):
    tok_rows, width = tokens.shape
    chips = lax.axis_size("y") * lax.axis_size("x")
    side = lax.axis_index("zh")
    flag = (lax.axis_index("c") == side).astype(jnp.int32).reshape(1)

    routes = jnp.concatenate([route_ids.astype(jnp.float32), route_gates], axis=1)
    high = lax.reduce_precision(route_gates, 8, 7)
    extra = jnp.concatenate([route_ids.astype(jnp.float32), high, route_gates - high], axis=1)
    extra = jnp.pad(extra.astype(jnp.bfloat16), ((0, 0), (0, 128 - extra.shape[1])))
    other = pair_exchange(jnp.concatenate([tokens, extra], axis=1))

    top = route_ids.shape[1]
    hosted = (2 * jnp.arange(chips, dtype=jnp.int32) + side).astype(jnp.float32)
    place = jnp.arange(tok_rows)
    earlier = (place[:, None] > place[None, :]).astype(jnp.bfloat16)

    def slots(table, shift):
        match = (table[:, :top, None] == hosted[None, None, :]).astype(jnp.float32)
        named = jnp.sum(match, axis=1)
        weight = jnp.sum(table[:, top:, None] * match, axis=1)
        rank = jnp.dot(earlier, named.astype(jnp.bfloat16), preferred_element_type=jnp.float32)
        rank = jnp.where(named > 0, rank.astype(jnp.int32), -1)[:, :, None]
        on_tile = rank == jnp.arange(16)
        on_rest = (rank - 16 + 4 * shift == jnp.arange(8)) & (rank >= 16)
        on_main = jnp.zeros_like(on_tile[:, :, :8])
        halves = [on_tile[:, :, :8], on_tile[:, :, 8:]]
        on_main = jnp.concatenate(
            [piece for half in halves for piece in ((on_main, half) if shift else (half, on_main))],
            axis=2,
        )
        return (
            *(jnp.transpose(on, (1, 2, 0)).astype(jnp.bfloat16) for on in (on_tile, on_rest)),
            *(jnp.where(on, weight[:, :, None], 0.0) for on in (on_main, on_rest)),
        )

    def rows_of(part, rows):
        flat = part.reshape(-1, rows.shape[0])
        return jnp.dot(flat, rows, preferred_element_type=jnp.float32).astype(jnp.bfloat16)

    def exchange_main(rows):
        parts = rows.reshape(2 * chips, -1, rows.shape[1])
        return lax.all_to_all(parts, EXP, 0, 0, tiled=True).reshape(rows.shape)

    def exchange_rest(rows):
        parts = rows.reshape(chips, 8, rows.shape[1])
        return lax.all_to_all(parts, ("y", "x"), 0, 0, tiled=True).reshape(rows.shape)

    pick, pick_rest, mix_own, mix_own_rest = slots(routes, 0)
    sent = rows_of(pick, tokens)
    mine = exchange_main(sent)
    other = after(other, sent)
    extra, other = other[:, width:].astype(jnp.float32), other[:, :width]
    ids, gate, low = (extra[:, at : at + 8] for at in (0, 8, 16))
    other_routes = jnp.concatenate([ids, gate + low], axis=1)

    gate_up = jnp.concatenate([after(gate_weight[0], other), up_weight[0]], axis=0)
    near = along(gate_up, NEXT)
    far = along(gate_up, FAR)

    pick, other_rest, mix_other, mix_other_rest = slots(other_routes, 1)
    theirs = exchange_main(after(rows_of(pick, other), mine))
    rest = rows_of(
        jnp.concatenate([pick_rest, other_rest], axis=2), jnp.concatenate([tokens, other], axis=0)
    )
    rest = exchange_rest(after(rest, theirs))
    copied, across = along(gate_up, FROM_HOME), along(after(near, theirs), SIBLING)

    def halves(*parts):
        part = jnp.concatenate([part.reshape(tok_rows, -1) for part in parts], axis=0)
        high = lax.reduce_precision(part, 8, 7)
        return jnp.concatenate([high, part - high], axis=0).astype(jnp.bfloat16)

    mix_main, mix_rest = halves(mix_own, mix_other), halves(mix_own_rest, mix_other_rest)
    count = 2 * tok_rows

    def columns(number, *earlier):
        at = sum(STEPS[:number])
        own = after(down_weight[0][:, at : at + STEPS[number]], *earlier)
        return own, along(own, NEXT), along(own, FAR)

    down_0 = columns(0, near)
    first = hidden_units(flag, mine, theirs, rest, [(gate_up, copied), (near,), (across,)])
    brought = along(after(far, first), TO_HOME)
    down_1 = columns(1, far, first)
    last = hidden_units(flag, after(mine, first), theirs, rest, [(brought, far)])
    result_0 = down_rows(flag, first, last, share(*down_0, first, first))
    down_2 = columns(2, down_0[2], result_0[0])
    result_1 = down_rows(flag, first, last, share(*down_1, result_0[0], result_0[0]))
    result_2 = down_rows(flag, first, last, share(*down_2, result_1[0], result_1[0]))
    mains, rests = zip(result_0, result_1, result_2, strict=True)
    early = jnp.concatenate(rests[:2], axis=1)
    back_0 = exchange_main(mains[0])
    early = exchange_rest(after(early, back_0))
    back_1 = exchange_main(after(mains[1], early))
    late = exchange_rest(after(rests[2], back_1))
    back_2 = exchange_main(after(mains[2], late))
    outs = []
    for back, back_rest in (
        (back_0, early[:, : STEPS[0]]),
        (back_1, early[:, STEPS[0] :]),
        (back_2, late),
    ):
        sums = jnp.dot(mix_main, back, preferred_element_type=jnp.float32) + jnp.dot(
            mix_rest, back_rest, preferred_element_type=jnp.float32
        )
        sums = sums[:count] + sums[count:]
        partner = pair_exchange(sums[tok_rows:].astype(jnp.bfloat16))
        outs.append((sums[:tok_rows] + partner.astype(jnp.float32)).astype(jnp.bfloat16))
    return jnp.concatenate(outs, axis=1)


def solution(mesh):
    fine = Mesh(mesh.devices.reshape(4, 4, 2, 2, 2), ALL)
    rows = P(ALL, None)
    panels = P(EXP, ("zh", "zl"), None)
    return jax.shard_map(
        body,
        mesh=fine,
        in_specs=(rows, rows, rows, panels, panels, panels),
        out_specs=rows,
        check_vma=False,
    )
```

```python
import functools

import jax
import jax.numpy as jnp
from jax import lax
from jax.experimental import pallas as pl
from jax.experimental.pallas import tpu as pltpu
from jax.sharding import Mesh, PartitionSpec as P

EXP = ("y", "x", "c")
COL = ("c", "zh", "zl")
ALL = ("y", "x", "c", "zh", "zl")


def swaps(*pairs):
    return [way for a, b in pairs for way in ((a, b), (b, a))]


PAIR = swaps((0, 3), (1, 2))
NEXT = swaps((0, 1), (6, 7), (4, 3), (5, 2))
FAR = swaps((5, 3), (4, 2))
SIBLING = swaps((0, 4), (1, 5), (2, 6), (3, 7))
FROM_HOME = [(0, 4), (1, 5), (6, 2), (7, 3)]
TO_HOME = [(b, a) for a, b in FROM_HOME]
STEPS = (1792, 2688, 2688)
QUARTER = 256
HALF = 128
MAIN = 256
REST = 128
TILE = 896
DEEP = 1792


def along(value, pairs):
    return lax.ppermute(value, COL, pairs)


def after(value, *earlier):
    return lax.optimization_barrier((value, *earlier))[0]


def share(near, far, earlier):
    across = along(after(near, earlier), SIBLING)
    brought = along(after(far, earlier), TO_HOME)
    return near, across, brought, far


def pick_block(flag, wanted, block):
    return jnp.where(flag[0] == wanted, block, 0)


def hidden_kernel(flag, mine, theirs, rest, *refs, kinds):
    panels, out, total = refs[:-2], refs[-2], refs[-1]
    part = pl.program_id(0)

    @pl.when(part == 0)
    def _():
        total[...] = jnp.zeros_like(total)

    at = 0
    for unit, kind in enumerate(kinds):
        panel = panels[at][...]
        if kind == 2:
            panel = jnp.where(flag[0] == 1, panel, panels[at + 1][...])
        for rows, first in ((mine, 0), (theirs, MAIN), (rest, 2 * MAIN)):
            total[pl.ds(first, rows.shape[0]), pl.ds(unit * 2 * HALF, 2 * HALF)] += lax.dot_general(
                rows[...], panel, (((1,), (1,)), ((), ())), preferred_element_type=jnp.float32
            )
        at += kind

    @pl.when(part == pl.num_programs(0) - 1)
    def _():
        for unit in range(len(kinds)):
            gate = total[:, pl.ds(unit * 2 * HALF, HALF)]
            upper = total[:, pl.ds(unit * 2 * HALF + HALF, HALF)]
            hidden = gate / (1.0 + jnp.exp(-gate)) * upper
            out[:, pl.ds(unit * HALF, HALF)] = hidden.astype(out.dtype)


def hidden_units(flag, mine, theirs, rest, units):
    rows, width = 2 * MAIN + REST, rest.shape[1]
    kinds = tuple(len(unit) for unit in units)
    specs = [pl.BlockSpec((part.shape[0], DEEP), lambda i, f: (0, i)) for part in (mine, theirs, rest)]
    operands = [mine, theirs, rest]
    for unit in units:
        for place, panel in enumerate(unit):
            if len(unit) == 1:
                spec = pl.BlockSpec((2 * HALF, DEEP), lambda i, f: (0, i))
            else:
                spec = pl.BlockSpec(
                    (2 * HALF, DEEP), lambda i, f, w=1 - place: (0, pick_block(f, w, i))
                )
            specs.append(spec)
            operands.append(panel)
    return pl.pallas_call(
        functools.partial(hidden_kernel, kinds=kinds),
        grid_spec=pltpu.PrefetchScalarGridSpec(
            num_scalar_prefetch=1,
            grid=(width // DEEP,),
            in_specs=specs,
            out_specs=pl.BlockSpec((rows, len(units) * HALF), lambda i, f: (0, 0)),
            scratch_shapes=[pltpu.VMEM((rows, len(units) * 2 * HALF), jnp.float32)],
        ),
        out_shape=jax.ShapeDtypeStruct((rows, len(units) * HALF), jnp.bfloat16),
        compiler_params=pltpu.CompilerParams(vmem_limit_bytes=48 * 2**20),
        cost_estimate=pl.CostEstimate(
            flops=4 * rows * width * len(units) * HALF,
            bytes_accessed=2 * width * (rows + 2 * len(units) * HALF),
            transcendentals=rows * len(units) * HALF,
        ),
    )(flag, *operands)


def down_kernel(flag, first, last, own, copied, near, across, brought, far, out_main, out_rest):
    home = flag[0] == 1
    panels = (
        (first[:, :QUARTER], jnp.where(home, own[...], copied[...])),
        (first[:, QUARTER : 2 * QUARTER], near[...]),
        (first[:, 2 * QUARTER : 3 * QUARTER], across[...]),
        (
            jnp.concatenate([first[:, 3 * QUARTER :], last[...]], axis=1),
            jnp.where(home, brought[...], far[...]),
        ),
    )
    total = None
    for hidden, weights in panels:
        term = jnp.dot(hidden, weights, preferred_element_type=jnp.float32)
        total = term if total is None else total + term
    total = total.astype(out_main.dtype)
    out_main[:, :8] = total[:MAIN].reshape(-1, 8, TILE)
    out_main[:, 8:] = total[MAIN : 2 * MAIN].reshape(-1, 8, TILE)
    out_rest[...] = total[2 * MAIN :]


def down_rows(flag, first, last, whole, at, panels):
    step = panels[0].shape[1]
    rows = 2 * MAIN + REST

    def panel(wanted=None, skip=0):
        if wanted is None:
            return pl.BlockSpec((QUARTER, TILE), lambda i, f: (0, i))
        return pl.BlockSpec(
            (QUARTER, TILE), lambda i, f: (0, pick_block(f, wanted, skip // TILE + i))
        )

    main, tail = pl.pallas_call(
        down_kernel,
        grid_spec=pltpu.PrefetchScalarGridSpec(
            num_scalar_prefetch=1,
            grid=(step // TILE,),
            in_specs=[
                pl.BlockSpec(first.shape, lambda i, f: (0, 0)),
                pl.BlockSpec(last.shape, lambda i, f: (0, 0)),
                panel(1, at),
                panel(0, at),
                panel(),
                panel(),
                panel(1),
                panel(0),
            ],
            out_specs=[
                pl.BlockSpec((MAIN // 8, 16, TILE), lambda i, f: (0, 0, i)),
                pl.BlockSpec((REST, TILE), lambda i, f: (0, i)),
            ],
        ),
        out_shape=[
            jax.ShapeDtypeStruct((MAIN // 8, 16, step), jnp.bfloat16),
            jax.ShapeDtypeStruct((REST, step), jnp.bfloat16),
        ],
        compiler_params=pltpu.CompilerParams(vmem_limit_bytes=32 * 2**20),
        cost_estimate=pl.CostEstimate(
            flops=8 * rows * QUARTER * step,
            bytes_accessed=2 * (4 * QUARTER * step + rows * (4 * QUARTER + step)),
            transcendentals=0,
        ),
    )(flag, first, last, *whole, *panels)
    return main.reshape(2 * MAIN, step), tail


def pair_exchange(value):
    return lax.ppermute(value, ("zh", "zl"), PAIR)


def body(tokens, route_ids, route_gates, gate_weight, up_weight, down_weight):
    tok_rows, width = tokens.shape
    chips = lax.axis_size("y") * lax.axis_size("x")
    side = lax.axis_index("zh")
    flag = (lax.axis_index("c") == side).astype(jnp.int32).reshape(1)

    routes = jnp.concatenate([route_ids.astype(jnp.float32), route_gates], axis=1)
    high = lax.reduce_precision(route_gates, 8, 7)
    extra = jnp.concatenate([route_ids.astype(jnp.float32), high, route_gates - high], axis=1)
    extra = jnp.pad(extra.astype(jnp.bfloat16), ((0, 0), (0, 128 - extra.shape[1])))
    other = pair_exchange(jnp.concatenate([tokens, extra], axis=1))

    top = route_ids.shape[1]
    hosted = (2 * jnp.arange(chips, dtype=jnp.int32) + side).astype(jnp.float32)
    place = jnp.arange(tok_rows)
    earlier = (place[:, None] > place[None, :]).astype(jnp.bfloat16)

    def slots(table, shift):
        match = (table[:, :top, None] == hosted[None, None, :]).astype(jnp.float32)
        named = jnp.sum(match, axis=1)
        weight = jnp.sum(table[:, top:, None] * match, axis=1)
        rank = jnp.dot(earlier, named.astype(jnp.bfloat16), preferred_element_type=jnp.float32)
        rank = jnp.where(named > 0, rank.astype(jnp.int32), -1)[:, :, None]
        on_tile = rank == jnp.arange(16)
        on_rest = (rank - 16 + 4 * shift == jnp.arange(8)) & (rank >= 16)
        on_main = jnp.zeros_like(on_tile[:, :, :8])
        halves = [on_tile[:, :, :8], on_tile[:, :, 8:]]
        on_main = jnp.concatenate(
            [piece for half in halves for piece in ((on_main, half) if shift else (half, on_main))],
            axis=2,
        )
        return (
            *(jnp.transpose(on, (1, 2, 0)).astype(jnp.bfloat16) for on in (on_tile, on_rest)),
            *(jnp.where(on, weight[:, :, None], 0.0) for on in (on_main, on_rest)),
        )

    def rows_of(part, rows):
        flat = part.reshape(-1, rows.shape[0])
        return jnp.dot(flat, rows, preferred_element_type=jnp.float32).astype(jnp.bfloat16)

    def exchange_main(rows):
        parts = rows.reshape(2 * chips, -1, rows.shape[1])
        return lax.all_to_all(parts, EXP, 0, 0, tiled=True).reshape(rows.shape)

    def exchange_rest(rows):
        parts = rows.reshape(chips, 8, rows.shape[1])
        return lax.all_to_all(parts, ("y", "x"), 0, 0, tiled=True).reshape(rows.shape)

    pick, pick_rest, mix_own, mix_own_rest = slots(routes, 0)
    sent = rows_of(pick, tokens)
    mine = exchange_main(sent)
    other = after(other, sent)
    extra, other = other[:, width:].astype(jnp.float32), other[:, :width]
    ids, gate, low = (extra[:, at : at + 8] for at in (0, 8, 16))
    other_routes = jnp.concatenate([ids, gate + low], axis=1)

    gate, upper = after(gate_weight[0], other), up_weight[0]
    owns = [
        jnp.concatenate([part[at : at + HALF] for part in (gate, upper)], axis=0)
        for at in (0, HALF)
    ]
    nears = [along(own, NEXT) for own in owns]
    fars = [along(owns[0], FAR), along(after(owns[1], *nears), FAR)]

    pick, other_rest, mix_other, mix_other_rest = slots(other_routes, 1)
    theirs = exchange_main(after(rows_of(pick, other), mine))
    rest = rows_of(
        jnp.concatenate([pick_rest, other_rest], axis=2), jnp.concatenate([tokens, other], axis=0)
    )
    rest = exchange_rest(after(rest, theirs))
    copied = [along(own, FROM_HOME) for own in owns]
    across = [along(after(near, theirs), SIBLING) for near in nears]
    brought_0 = along(after(fars[0], theirs), TO_HOME)

    def halves(*parts):
        part = jnp.concatenate([part.reshape(tok_rows, -1) for part in parts], axis=0)
        high = lax.reduce_precision(part, 8, 7)
        return jnp.concatenate([high, part - high], axis=0).astype(jnp.bfloat16)

    mix_main, mix_rest = halves(mix_own, mix_other), halves(mix_own_rest, mix_other_rest)
    count = 2 * tok_rows

    def columns(at, step, *earlier):
        own = after(down_weight[0][:, at : at + step], *earlier)
        return along(own, NEXT), along(own, FAR)

    whole = down_weight[0], along(after(down_weight[0], *copied), FROM_HOME)
    down_0 = columns(0, STEPS[0], *nears)
    units = [*zip(owns, copied, strict=True), *zip(nears), *zip(across), (brought_0, fars[0])]
    first = hidden_units(flag, after(mine, whole[1]), theirs, rest, units)
    brought_1 = along(after(fars[1], first), TO_HOME)
    down_1 = columns(STEPS[0], STEPS[1], fars[1], first)
    last = hidden_units(flag, after(mine, first), theirs, rest, [(brought_1, fars[1])])
    result_0 = down_rows(flag, first, last, whole, 0, share(*down_0, first))
    down_2 = columns(STEPS[0] + STEPS[1], STEPS[2], down_0[1], result_0[0])
    result_1 = down_rows(flag, first, last, whole, STEPS[0], share(*down_1, result_0[0]))
    result_2 = down_rows(
        flag, first, last, whole, STEPS[0] + STEPS[1], share(*down_2, result_1[0])
    )
    mains, rests = zip(result_0, result_1, result_2, strict=True)
    early = jnp.concatenate(rests[:2], axis=1)
    back_0 = exchange_main(mains[0])
    early = exchange_rest(after(early, back_0))
    back_1 = exchange_main(after(mains[1], early))
    late = exchange_rest(after(rests[2], back_1))
    back_2 = exchange_main(after(mains[2], late))
    outs = []
    for back, back_rest in (
        (back_0, early[:, : STEPS[0]]),
        (back_1, early[:, STEPS[0] :]),
        (back_2, late),
    ):
        sums = jnp.dot(mix_main, back, preferred_element_type=jnp.float32) + jnp.dot(
            mix_rest, back_rest, preferred_element_type=jnp.float32
        )
        sums = sums[:count] + sums[count:]
        partner = pair_exchange(sums[tok_rows:].astype(jnp.bfloat16))
        outs.append((sums[:tok_rows] + partner.astype(jnp.float32)).astype(jnp.bfloat16))
    return jnp.concatenate(outs, axis=1)


def solution(mesh):
    fine = Mesh(mesh.devices.reshape(4, 4, 2, 2, 2), ALL)
    rows = P(ALL, None)
    panels = P(EXP, ("zh", "zl"), None)
    return jax.shard_map(
        body,
        mesh=fine,
        in_specs=(rows, rows, rows, panels, panels, panels),
        out_specs=rows,
        check_vma=False,
    )
```

```python
import functools

import jax
import jax.numpy as jnp
from jax import lax
from jax.experimental import pallas as pl
from jax.experimental.pallas import tpu as pltpu
from jax.sharding import Mesh, PartitionSpec as P

EXP = ("y", "x", "c")
COL = ("c", "zh", "zl")
ALL = ("y", "x", "c", "zh", "zl")


def swaps(*pairs):
    return [way for a, b in pairs for way in ((a, b), (b, a))]


PAIR = swaps((0, 3), (1, 2))
NEXT = swaps((0, 1), (6, 7), (4, 3), (5, 2))
FAR = swaps((5, 3), (4, 2))
SIBLING = swaps((0, 4), (1, 5), (2, 6), (3, 7))
FROM_HOME = [(0, 4), (1, 5), (6, 2), (7, 3)]
TO_HOME = [(b, a) for a, b in FROM_HOME]
STEPS = (1792, 2688, 2688)
QUARTER = 256
HALF = 128
MAIN = 256
REST = 128
TILE = 896
DEEP = 1792


def along(value, pairs):
    return lax.ppermute(value, COL, pairs)


def after(value, *earlier):
    return lax.optimization_barrier((value, *earlier))[0]


def share(near, far, earlier):
    across = along(after(near, earlier), SIBLING)
    brought = along(after(far, earlier), TO_HOME)
    return near, across, brought, far


def pick_block(flag, wanted, block):
    return jnp.where(flag[0] == wanted, block, 0)


def hidden_kernel(flag, mine, theirs, rest, *refs, kinds):
    panels, out, total = refs[:-2], refs[-2], refs[-1]
    part = pl.program_id(0)

    @pl.when(part == 0)
    def _():
        total[...] = jnp.zeros_like(total)

    at = 0
    for unit, kind in enumerate(kinds):
        panel = panels[at][...]
        if kind == 2:
            panel = jnp.where(flag[0] == 1, panel, panels[at + 1][...])
        for rows, first in ((mine, 0), (theirs, MAIN), (rest, 2 * MAIN)):
            total[pl.ds(first, rows.shape[0]), pl.ds(unit * 2 * HALF, 2 * HALF)] += lax.dot_general(
                rows[...], panel, (((1,), (1,)), ((), ())), preferred_element_type=jnp.float32
            )
        at += kind

    @pl.when(part == pl.num_programs(0) - 1)
    def _():
        for unit in range(len(kinds)):
            gate = total[:, pl.ds(unit * 2 * HALF, HALF)]
            upper = total[:, pl.ds(unit * 2 * HALF + HALF, HALF)]
            hidden = gate / (1.0 + jnp.exp(-gate)) * upper
            out[:, pl.ds(unit * HALF, HALF)] = hidden.astype(out.dtype)


def hidden_units(flag, mine, theirs, rest, units):
    rows, width = 2 * MAIN + REST, rest.shape[1]
    kinds = tuple(len(unit) for unit in units)
    specs = [pl.BlockSpec((part.shape[0], DEEP), lambda i, f: (0, i)) for part in (mine, theirs, rest)]
    operands = [mine, theirs, rest]
    for unit in units:
        for place, panel in enumerate(unit):
            if len(unit) == 1:
                spec = pl.BlockSpec((2 * HALF, DEEP), lambda i, f: (0, i))
            else:
                spec = pl.BlockSpec(
                    (2 * HALF, DEEP), lambda i, f, w=1 - place: (0, pick_block(f, w, i))
                )
            specs.append(spec)
            operands.append(panel)
    return pl.pallas_call(
        functools.partial(hidden_kernel, kinds=kinds),
        grid_spec=pltpu.PrefetchScalarGridSpec(
            num_scalar_prefetch=1,
            grid=(width // DEEP,),
            in_specs=specs,
            out_specs=pl.BlockSpec((rows, len(units) * HALF), lambda i, f: (0, 0)),
            scratch_shapes=[pltpu.VMEM((rows, len(units) * 2 * HALF), jnp.float32)],
        ),
        out_shape=jax.ShapeDtypeStruct((rows, len(units) * HALF), jnp.bfloat16),
        compiler_params=pltpu.CompilerParams(vmem_limit_bytes=48 * 2**20),
        cost_estimate=pl.CostEstimate(flops=1, bytes_accessed=1, transcendentals=0),
    )(flag, *operands)


def down_kernel(flag, first, last, own, copied, near, across, brought, far, out_main, out_rest):
    home = flag[0] == 1
    panels = (
        (first[:, :QUARTER], jnp.where(home, own[...], copied[...])),
        (first[:, QUARTER : 2 * QUARTER], near[...]),
        (first[:, 2 * QUARTER : 3 * QUARTER], across[...]),
        (
            jnp.concatenate([first[:, 3 * QUARTER :], last[...]], axis=1),
            jnp.where(home, brought[...], far[...]),
        ),
    )
    total = None
    for hidden, weights in panels:
        term = jnp.dot(hidden, weights, preferred_element_type=jnp.float32)
        total = term if total is None else total + term
    total = total.astype(out_main.dtype)
    out_main[:, :8] = total[:MAIN].reshape(-1, 8, TILE)
    out_main[:, 8:] = total[MAIN : 2 * MAIN].reshape(-1, 8, TILE)
    out_rest[...] = total[2 * MAIN :]


def down_rows(flag, first, last, panels, step, starts):
    rows = 2 * MAIN + REST

    def panel(wanted, start):
        skip = start // TILE
        if wanted is None:
            return pl.BlockSpec((QUARTER, TILE), lambda i, f: (0, skip + i))
        return pl.BlockSpec((QUARTER, TILE), lambda i, f: (0, pick_block(f, wanted, skip + i)))

    main, tail = pl.pallas_call(
        down_kernel,
        grid_spec=pltpu.PrefetchScalarGridSpec(
            num_scalar_prefetch=1,
            grid=(step // TILE,),
            in_specs=[
                pl.BlockSpec(first.shape, lambda i, f: (0, 0)),
                pl.BlockSpec(last.shape, lambda i, f: (0, 0)),
                *map(panel, (1, 0, None, None, 1, 0), starts),
            ],
            out_specs=[
                pl.BlockSpec((MAIN // 8, 16, TILE), lambda i, f: (0, 0, i)),
                pl.BlockSpec((REST, TILE), lambda i, f: (0, i)),
            ],
        ),
        out_shape=[
            jax.ShapeDtypeStruct((MAIN // 8, 16, step), jnp.bfloat16),
            jax.ShapeDtypeStruct((REST, step), jnp.bfloat16),
        ],
        compiler_params=pltpu.CompilerParams(vmem_limit_bytes=32 * 2**20),
        cost_estimate=pl.CostEstimate(
            flops=8 * rows * QUARTER * step,
            bytes_accessed=2 * (4 * QUARTER * step + rows * (4 * QUARTER + step)),
            transcendentals=0,
        ),
    )(flag, first, last, *panels)
    return main.reshape(2 * MAIN, step), tail


def pair_exchange(value):
    return lax.ppermute(value, ("zh", "zl"), PAIR)


def body(tokens, route_ids, route_gates, gate_weight, up_weight, down_weight):
    tok_rows, width = tokens.shape
    chips = lax.axis_size("y") * lax.axis_size("x")
    side = lax.axis_index("zh")
    flag = (lax.axis_index("c") == side).astype(jnp.int32).reshape(1)

    routes = jnp.concatenate([route_ids.astype(jnp.float32), route_gates], axis=1)
    high = lax.reduce_precision(route_gates, 8, 7)
    extra = jnp.concatenate([route_ids.astype(jnp.float32), high, route_gates - high], axis=1)
    extra = jnp.pad(extra.astype(jnp.bfloat16), ((0, 0), (0, 128 - extra.shape[1])))
    other = pair_exchange(jnp.concatenate([tokens, extra], axis=1))

    top = route_ids.shape[1]
    hosted = (2 * jnp.arange(chips, dtype=jnp.int32) + side).astype(jnp.float32)
    place = jnp.arange(tok_rows)
    earlier = (place[:, None] > place[None, :]).astype(jnp.bfloat16)

    def slots(table, shift):
        match = (table[:, :top, None] == hosted[None, None, :]).astype(jnp.float32)
        named = jnp.sum(match, axis=1)
        weight = jnp.sum(table[:, top:, None] * match, axis=1)
        rank = jnp.dot(earlier, named.astype(jnp.bfloat16), preferred_element_type=jnp.float32)
        rank = jnp.where(named > 0, rank.astype(jnp.int32), -1)[:, :, None]
        on_tile = rank == jnp.arange(16)
        on_rest = (rank - 16 + 4 * shift == jnp.arange(8)) & (rank >= 16)
        on_main = jnp.zeros_like(on_tile[:, :, :8])
        halves = [on_tile[:, :, :8], on_tile[:, :, 8:]]
        on_main = jnp.concatenate(
            [piece for half in halves for piece in ((on_main, half) if shift else (half, on_main))],
            axis=2,
        )
        return (
            *(jnp.transpose(on, (1, 2, 0)).astype(jnp.bfloat16) for on in (on_tile, on_rest)),
            *(jnp.where(on, weight[:, :, None], 0.0) for on in (on_main, on_rest)),
        )

    def rows_of(part, rows):
        flat = part.reshape(-1, rows.shape[0])
        return jnp.dot(flat, rows, preferred_element_type=jnp.float32).astype(jnp.bfloat16)

    def exchange_main(rows):
        parts = rows.reshape(2 * chips, -1, rows.shape[1])
        return lax.all_to_all(parts, EXP, 0, 0, tiled=True).reshape(rows.shape)

    def exchange_rest(rows):
        parts = rows.reshape(chips, 8, rows.shape[1])
        return lax.all_to_all(parts, ("y", "x"), 0, 0, tiled=True).reshape(rows.shape)

    pick, pick_rest, mix_own, mix_own_rest = slots(routes, 0)
    sent = rows_of(pick, tokens)
    mine = exchange_main(sent)
    other = after(other, sent)
    extra, other = other[:, width:].astype(jnp.float32), other[:, :width]
    ids, gate, low = (extra[:, at : at + 8] for at in (0, 8, 16))
    other_routes = jnp.concatenate([ids, gate + low], axis=1)

    owns = [
        jnp.concatenate(
            [after(gate_weight[0], got)[at : at + HALF], up_weight[0][at : at + HALF]], axis=0
        )
        for at, got in ((0, sent), (HALF, other))
    ]
    owns[1] = jnp.concatenate([owns[1], down_weight[0][:, : STEPS[0]]], axis=1)
    nears = [along(own, NEXT) for own in owns]

    pick, other_rest, mix_other, mix_other_rest = slots(other_routes, 1)
    rest = rows_of(
        jnp.concatenate([pick_rest, other_rest], axis=2), jnp.concatenate([tokens, other], axis=0)
    )
    theirs = exchange_main(after(rows_of(pick, other), mine, nears[0]))
    rest = exchange_rest(after(rest, theirs))
    fars = [along(owns[0], FAR), along(after(owns[1], nears[0], theirs), FAR)]
    copied = [along(own, FROM_HOME) for own in owns]
    across = [
        along(after(near, got), SIBLING) for near, got in zip(nears, (theirs, rest), strict=True)
    ]
    brought_0 = along(after(fars[0], rest), TO_HOME)

    def halves(*parts):
        part = jnp.concatenate([part.reshape(tok_rows, -1) for part in parts], axis=0)
        high = lax.reduce_precision(part, 8, 7)
        return jnp.concatenate([high, part - high], axis=0).astype(jnp.bfloat16)

    mix_main, mix_rest = halves(mix_own, mix_other), halves(mix_own_rest, mix_other_rest)
    count = 2 * tok_rows

    def columns(at, step, *earlier):
        own = after(down_weight[0][:, at : at + step], *earlier)
        return along(own, NEXT), along(own, FAR)

    whole = down_weight[0], along(after(down_weight[0], *copied), FROM_HOME)
    units = [*zip(owns, copied, strict=True), *zip(nears), *zip(across), (brought_0, fars[0])]
    first = hidden_units(flag, after(mine, whole[1]), theirs, rest, units)
    brought_1 = along(after(fars[1], first), TO_HOME)
    down_1 = columns(STEPS[0], STEPS[1], fars[1], first)
    last = hidden_units(flag, after(mine, first), theirs, rest, [(brought_1, fars[1])])
    panels = owns[1], copied[1], nears[1], across[1], brought_1, fars[1]
    result_0 = down_rows(flag, first, last, panels, STEPS[0], (width,) * 6)
    at = STEPS[0] + STEPS[1]
    down_2 = columns(at, STEPS[2], down_1[1], result_0[0])
    panels = whole + share(*down_1, result_0[0])
    result_1 = down_rows(flag, first, last, panels, STEPS[1], (STEPS[0],) * 2 + (0,) * 4)
    panels = whole + share(*down_2, result_1[0])
    result_2 = down_rows(flag, first, last, panels, STEPS[2], (at,) * 2 + (0,) * 4)
    mains, rests = zip(result_0, result_1, result_2, strict=True)
    back_0 = exchange_main(mains[0])
    back_1 = exchange_main(after(mains[1], back_0))
    back_rest = exchange_rest(after(jnp.concatenate(rests, axis=1), back_1))
    back_2 = exchange_main(after(mains[2], back_rest))
    outs, at = [], 0
    for back in (back_0, back_1, back_2):
        tail = back_rest[:, at : at + back.shape[1]]
        at += back.shape[1]
        sums = jnp.dot(mix_main, back, preferred_element_type=jnp.float32) + jnp.dot(
            mix_rest, tail, preferred_element_type=jnp.float32
        )
        sums = sums[:count] + sums[count:]
        partner = pair_exchange(sums[tok_rows:].astype(jnp.bfloat16))
        outs.append((sums[:tok_rows] + partner.astype(jnp.float32)).astype(jnp.bfloat16))
    return jnp.concatenate(outs, axis=1)


def solution(mesh):
    fine = Mesh(mesh.devices.reshape(4, 4, 2, 2, 2), ALL)
    rows = P(ALL, None)
    panels = P(EXP, ("zh", "zl"), None)
    return jax.shard_map(
        body,
        mesh=fine,
        in_specs=(rows, rows, rows, panels, panels, panels),
        out_specs=rows,
        check_vma=False,
    )
```

```python
import functools

import jax
import jax.numpy as jnp
from jax import lax
from jax.experimental import pallas as pl
from jax.experimental.pallas import tpu as pltpu
from jax.sharding import Mesh, PartitionSpec as P

EXP = ("y", "x", "c")
COL = ("c", "zh", "zl")
ALL = ("y", "x", "c", "zh", "zl")


def swaps(*pairs):
    return [way for a, b in pairs for way in ((a, b), (b, a))]


PAIR = swaps((0, 3), (1, 2))
NEXT = swaps((0, 1), (6, 7), (4, 3), (5, 2))
FAR = swaps((5, 3), (4, 2))
SIBLING = swaps((0, 4), (1, 5), (2, 6), (3, 7))
FROM_HOME = [(0, 4), (1, 5), (6, 2), (7, 3)]
TO_HOME = [(b, a) for a, b in FROM_HOME]
STEPS = (1792, 2688, 2688)
QUARTER = 256
HALF = 128
MAIN = 256
REST = 128
TILE = 896
DEEP = 1792


def along(value, pairs):
    return lax.ppermute(value, COL, pairs)


def after(value, *earlier):
    return lax.optimization_barrier((value, *earlier))[0]


def share(near, far, earlier):
    across = along(after(near, earlier), SIBLING)
    brought = along(after(far, earlier), TO_HOME)
    return near, across, brought, far


def pick_block(flag, wanted, block):
    return jnp.where(flag[0] == wanted, block, 0)


def hidden_kernel(flag, mine, theirs, rest, *refs, kinds):
    panels, out, total = refs[:-2], refs[-2], refs[-1]
    part = pl.program_id(0)

    @pl.when(part == 0)
    def _():
        total[...] = jnp.zeros_like(total)

    at = 0
    for unit, kind in enumerate(kinds):
        panel = panels[at][...]
        if kind == 2:
            panel = jnp.where(flag[0] == 1, panel, panels[at + 1][...])
        for rows, first in ((mine, 0), (theirs, MAIN), (rest, 2 * MAIN)):
            total[pl.ds(first, rows.shape[0]), pl.ds(unit * 2 * HALF, 2 * HALF)] += lax.dot_general(
                rows[...], panel, (((1,), (1,)), ((), ())), preferred_element_type=jnp.float32
            )
        at += kind

    @pl.when(part == pl.num_programs(0) - 1)
    def _():
        for unit in range(len(kinds)):
            gate = total[:, pl.ds(unit * 2 * HALF, HALF)]
            upper = total[:, pl.ds(unit * 2 * HALF + HALF, HALF)]
            hidden = gate / (1.0 + jnp.exp(-gate)) * upper
            out[:, pl.ds(unit * HALF, HALF)] = hidden.astype(out.dtype)


def hidden_units(flag, mine, theirs, rest, units):
    rows, width = 2 * MAIN + REST, rest.shape[1]
    kinds = tuple(len(unit) for unit in units)
    specs = [pl.BlockSpec((part.shape[0], DEEP), lambda i, f: (0, i)) for part in (mine, theirs, rest)]
    operands = [mine, theirs, rest]
    for unit in units:
        for place, panel in enumerate(unit):
            if len(unit) == 1:
                spec = pl.BlockSpec((2 * HALF, DEEP), lambda i, f: (0, i))
            else:
                spec = pl.BlockSpec(
                    (2 * HALF, DEEP), lambda i, f, w=1 - place: (0, pick_block(f, w, i))
                )
            specs.append(spec)
            operands.append(panel)
    return pl.pallas_call(
        functools.partial(hidden_kernel, kinds=kinds),
        grid_spec=pltpu.PrefetchScalarGridSpec(
            num_scalar_prefetch=1,
            grid=(width // DEEP,),
            in_specs=specs,
            out_specs=pl.BlockSpec((rows, len(units) * HALF), lambda i, f: (0, 0)),
            scratch_shapes=[pltpu.VMEM((rows, len(units) * 2 * HALF), jnp.float32)],
        ),
        out_shape=jax.ShapeDtypeStruct((rows, len(units) * HALF), jnp.bfloat16),
        compiler_params=pltpu.CompilerParams(vmem_limit_bytes=48 * 2**20),
        cost_estimate=pl.CostEstimate(flops=1, bytes_accessed=1, transcendentals=0),
    )(flag, *operands)


def down_kernel(flag, first, last, own, copied, near, across, brought, far, out_main, out_rest):
    home = flag[0] == 1
    panels = (
        (first[:, :QUARTER], jnp.where(home, own[...], copied[...])),
        (first[:, QUARTER : 2 * QUARTER], near[...]),
        (first[:, 2 * QUARTER : 3 * QUARTER], across[...]),
        (
            jnp.concatenate([first[:, 3 * QUARTER :], last[...]], axis=1),
            jnp.where(home, brought[...], far[...]),
        ),
    )
    total = None
    for hidden, weights in panels:
        term = jnp.dot(hidden, weights, preferred_element_type=jnp.float32)
        total = term if total is None else total + term
    total = total.astype(out_main.dtype)
    out_main[:, :8] = total[:MAIN].reshape(-1, 8, TILE)
    out_main[:, 8:] = total[MAIN : 2 * MAIN].reshape(-1, 8, TILE)
    out_rest[...] = total[2 * MAIN :]


def down_rows(flag, first, last, panels, step, starts):
    rows = 2 * MAIN + REST

    def panel(wanted, start):
        skip = start // TILE
        if wanted is None:
            return pl.BlockSpec((QUARTER, TILE), lambda i, f: (0, skip + i))
        return pl.BlockSpec((QUARTER, TILE), lambda i, f: (0, pick_block(f, wanted, skip + i)))

    main, tail = pl.pallas_call(
        down_kernel,
        grid_spec=pltpu.PrefetchScalarGridSpec(
            num_scalar_prefetch=1,
            grid=(step // TILE,),
            in_specs=[
                pl.BlockSpec(first.shape, lambda i, f: (0, 0)),
                pl.BlockSpec(last.shape, lambda i, f: (0, 0)),
                *map(panel, (1, 0, None, None, 1, 0), starts),
            ],
            out_specs=[
                pl.BlockSpec((MAIN // 8, 16, TILE), lambda i, f: (0, 0, i)),
                pl.BlockSpec((REST, TILE), lambda i, f: (0, i)),
            ],
        ),
        out_shape=[
            jax.ShapeDtypeStruct((MAIN // 8, 16, step), jnp.bfloat16),
            jax.ShapeDtypeStruct((REST, step), jnp.bfloat16),
        ],
        compiler_params=pltpu.CompilerParams(vmem_limit_bytes=32 * 2**20),
        cost_estimate=pl.CostEstimate(
            flops=8 * rows * QUARTER * step,
            bytes_accessed=2 * (4 * QUARTER * step + rows * (4 * QUARTER + step)),
            transcendentals=0,
        ),
    )(flag, first, last, *panels)
    return main.reshape(2 * MAIN, step), tail


def pair_exchange(value):
    return lax.ppermute(value, ("zh", "zl"), PAIR)


def body(tokens, route_ids, route_gates, gate_weight, up_weight, down_weight):
    tok_rows, width = tokens.shape
    chips = lax.axis_size("y") * lax.axis_size("x")
    side = lax.axis_index("zh")
    flag = (lax.axis_index("c") == side).astype(jnp.int32).reshape(1)

    routes = jnp.concatenate([route_ids.astype(jnp.float32), route_gates], axis=1)
    high = lax.reduce_precision(route_gates, 8, 7)
    extra = jnp.concatenate([route_ids.astype(jnp.float32), high, route_gates - high], axis=1)
    extra = jnp.pad(extra.astype(jnp.bfloat16), ((0, 0), (0, 128 - extra.shape[1])))
    other = pair_exchange(jnp.concatenate([tokens, extra], axis=1))

    top = route_ids.shape[1]
    hosted = (2 * jnp.arange(chips, dtype=jnp.int32) + side).astype(jnp.float32)
    place = jnp.arange(tok_rows)
    earlier = (place[:, None] > place[None, :]).astype(jnp.bfloat16)

    def slots(table, shift):
        match = (table[:, :top, None] == hosted[None, None, :]).astype(jnp.float32)
        named = jnp.sum(match, axis=1)
        weight = jnp.sum(table[:, top:, None] * match, axis=1)
        rank = jnp.dot(earlier, named.astype(jnp.bfloat16), preferred_element_type=jnp.float32)
        rank = jnp.where(named > 0, rank.astype(jnp.int32), -1)[:, :, None]
        on_tile = rank == jnp.arange(16)
        on_rest = (rank - 16 + 4 * shift == jnp.arange(8)) & (rank >= 16)
        on_main = jnp.zeros_like(on_tile[:, :, :8])
        halves = [on_tile[:, :, :8], on_tile[:, :, 8:]]
        on_main = jnp.concatenate(
            [piece for half in halves for piece in ((on_main, half) if shift else (half, on_main))],
            axis=2,
        )
        return (
            *(jnp.transpose(on, (1, 2, 0)).astype(jnp.bfloat16) for on in (on_tile, on_rest)),
            *(jnp.where(on, weight[:, :, None], 0.0) for on in (on_main, on_rest)),
        )

    def rows_of(part, rows):
        flat = part.reshape(-1, rows.shape[0])
        return jnp.dot(flat, rows, preferred_element_type=jnp.float32).astype(jnp.bfloat16)

    def exchange_main(rows):
        parts = rows.reshape(2 * chips, -1, rows.shape[1])
        return lax.all_to_all(parts, EXP, 0, 0, tiled=True).reshape(rows.shape)

    def exchange_rest(rows):
        parts = rows.reshape(chips, 8, rows.shape[1])
        return lax.all_to_all(parts, ("y", "x"), 0, 0, tiled=True).reshape(rows.shape)

    pick, pick_rest, mix_own, mix_own_rest = slots(routes, 0)
    sent = rows_of(pick, tokens)
    mine = exchange_main(sent)
    other = after(other, sent)
    extra, other = other[:, width:].astype(jnp.float32), other[:, :width]
    ids, gate, low = (extra[:, at : at + 8] for at in (0, 8, 16))
    other_routes = jnp.concatenate([ids, gate + low], axis=1)

    owns = [
        jnp.concatenate(
            [after(gate_weight[0], got)[at : at + HALF], up_weight[0][at : at + HALF]], axis=0
        )
        for at, got in ((0, other), (HALF, other))
    ]
    owns[0] = jnp.concatenate([owns[0], down_weight[0][:, : STEPS[0]]], axis=1)
    nears = [along(own, NEXT) for own in owns]

    pick, other_rest, mix_other, mix_other_rest = slots(other_routes, 1)
    rest = rows_of(
        jnp.concatenate([pick_rest, other_rest], axis=2), jnp.concatenate([tokens, other], axis=0)
    )
    theirs = exchange_main(after(rows_of(pick, other), mine, nears[0]))
    rest = exchange_rest(after(rest, theirs))
    fars = [along(owns[0], FAR), along(after(owns[1], nears[0], theirs), FAR)]
    copied = [along(own, FROM_HOME) for own in owns]
    across = [
        along(after(near, got), SIBLING) for near, got in zip(nears, (theirs, rest), strict=True)
    ]
    brought_0 = along(after(fars[0], rest), TO_HOME)

    def halves(*parts):
        part = jnp.concatenate([part.reshape(tok_rows, -1) for part in parts], axis=0)
        high = lax.reduce_precision(part, 8, 7)
        return jnp.concatenate([high, part - high], axis=0).astype(jnp.bfloat16)

    mix_main, mix_rest = halves(mix_own, mix_other), halves(mix_own_rest, mix_other_rest)
    count = 2 * tok_rows

    def columns(at, step, *earlier):
        own = after(down_weight[0][:, at : at + step], *earlier)
        return along(own, NEXT), along(own, FAR)

    whole = down_weight[0], along(after(down_weight[0], *copied), FROM_HOME)
    units = [*zip(owns, copied, strict=True), *zip(nears), *zip(across), (brought_0, fars[0])]
    first = hidden_units(flag, after(mine, whole[1]), theirs, rest, units)
    brought_1 = along(after(fars[1], first), TO_HOME)
    down_1 = columns(STEPS[0], STEPS[1], fars[1], first)
    last = hidden_units(flag, after(mine, first), theirs, rest, [(brought_1, fars[1])])
    panels = owns[0], copied[0], nears[0], across[0], brought_0, fars[0]
    result_0 = down_rows(flag, first, last, panels, STEPS[0], (width,) * 6)
    at = STEPS[0] + STEPS[1]
    down_2 = columns(at, STEPS[2], down_1[1], result_0[0])
    panels = whole + share(*down_1, result_0[0])
    result_1 = down_rows(flag, first, last, panels, STEPS[1], (STEPS[0],) * 2 + (0,) * 4)
    panels = whole + share(*down_2, result_1[0])
    result_2 = down_rows(flag, first, last, panels, STEPS[2], (at,) * 2 + (0,) * 4)
    mains, rests = zip(result_0, result_1, result_2, strict=True)
    back_0 = exchange_main(mains[0])
    back_1 = exchange_main(after(mains[1], back_0))
    back_rest = exchange_rest(after(jnp.concatenate(rests, axis=1), back_1))
    back_2 = exchange_main(after(mains[2], back_rest))
    outs, at = [], 0
    for back in (back_0, back_1, back_2):
        tail = back_rest[:, at : at + back.shape[1]]
        at += back.shape[1]
        sums = jnp.dot(mix_main, back, preferred_element_type=jnp.float32) + jnp.dot(
            mix_rest, tail, preferred_element_type=jnp.float32
        )
        sums = sums[:count] + sums[count:]
        partner = pair_exchange(sums[tok_rows:].astype(jnp.bfloat16))
        outs.append((sums[:tok_rows] + partner.astype(jnp.float32)).astype(jnp.bfloat16))
    return jnp.concatenate(outs, axis=1)


def solution(mesh):
    fine = Mesh(mesh.devices.reshape(4, 4, 2, 2, 2), ALL)
    rows = P(ALL, None)
    panels = P(EXP, ("zh", "zl"), None)
    return jax.shard_map(
        body,
        mesh=fine,
        in_specs=(rows, rows, rows, panels, panels, panels),
        out_specs=rows,
        check_vma=False,
    )
```

```python
import functools

import jax
import jax.numpy as jnp
from jax import lax
from jax.experimental import pallas as pl
from jax.experimental.pallas import tpu as pltpu
from jax.sharding import Mesh, PartitionSpec as P

EXP = ("y", "x", "c")
COL = ("c", "zh", "zl")
ALL = ("y", "x", "c", "zh", "zl")


def swaps(*pairs):
    return [way for a, b in pairs for way in ((a, b), (b, a))]


PAIR = swaps((0, 3), (1, 2))
NEXT = swaps((0, 1), (6, 7), (4, 3), (5, 2))
FAR = swaps((5, 3), (4, 2))
SIBLING = swaps((0, 4), (1, 5), (2, 6), (3, 7))
FROM_HOME = [(0, 4), (1, 5), (6, 2), (7, 3)]
TO_HOME = [(b, a) for a, b in FROM_HOME]
STEPS = (1792, 2688, 2688)
QUARTER = 256
HALF = 128
MAIN = 256
REST = 128
TILE = 896
DEEP = 1792


def along(value, pairs):
    return lax.ppermute(value, COL, pairs)


def after(value, *earlier):
    return lax.optimization_barrier((value, *earlier))[0]


def share(near, far, earlier):
    across = along(after(near, earlier), SIBLING)
    brought = along(after(far, earlier), TO_HOME)
    return near, across, brought, far


def pick_block(flag, wanted, block):
    return jnp.where(flag[0] == wanted, block, 0)


def hidden_kernel(flag, mine, theirs, rest, *refs, kinds):
    panels, out, total = refs[:-2], refs[-2], refs[-1]
    part = pl.program_id(0)

    @pl.when(part == 0)
    def _():
        total[...] = jnp.zeros_like(total)

    at = 0
    for unit, kind in enumerate(kinds):
        panel = panels[at][...]
        if kind == 2:
            panel = jnp.where(flag[0] == 1, panel, panels[at + 1][...])
        for rows, first in ((mine, 0), (theirs, MAIN), (rest, 2 * MAIN)):
            total[pl.ds(first, rows.shape[0]), pl.ds(unit * 2 * HALF, 2 * HALF)] += lax.dot_general(
                rows[...], panel, (((1,), (1,)), ((), ())), preferred_element_type=jnp.float32
            )
        at += kind

    @pl.when(part == pl.num_programs(0) - 1)
    def _():
        for unit in range(len(kinds)):
            gate = total[:, pl.ds(unit * 2 * HALF, HALF)]
            upper = total[:, pl.ds(unit * 2 * HALF + HALF, HALF)]
            hidden = gate / (1.0 + jnp.exp(-gate)) * upper
            out[:, pl.ds(unit * HALF, HALF)] = hidden.astype(out.dtype)


def hidden_units(flag, mine, theirs, rest, units):
    rows, width = 2 * MAIN + REST, rest.shape[1]
    kinds = tuple(len(unit) for unit in units)
    specs = [pl.BlockSpec((part.shape[0], DEEP), lambda i, f: (0, i)) for part in (mine, theirs, rest)]
    operands = [mine, theirs, rest]
    for unit in units:
        for place, panel in enumerate(unit):
            if len(unit) == 1:
                spec = pl.BlockSpec((2 * HALF, DEEP), lambda i, f: (0, i))
            else:
                spec = pl.BlockSpec(
                    (2 * HALF, DEEP), lambda i, f, w=1 - place: (0, pick_block(f, w, i))
                )
            specs.append(spec)
            operands.append(panel)
    return pl.pallas_call(
        functools.partial(hidden_kernel, kinds=kinds),
        grid_spec=pltpu.PrefetchScalarGridSpec(
            num_scalar_prefetch=1,
            grid=(width // DEEP,),
            in_specs=specs,
            out_specs=pl.BlockSpec((rows, len(units) * HALF), lambda i, f: (0, 0)),
            scratch_shapes=[pltpu.VMEM((rows, len(units) * 2 * HALF), jnp.float32)],
        ),
        out_shape=jax.ShapeDtypeStruct((rows, len(units) * HALF), jnp.bfloat16),
        compiler_params=pltpu.CompilerParams(vmem_limit_bytes=48 * 2**20),
        cost_estimate=pl.CostEstimate(flops=1, bytes_accessed=1, transcendentals=0),
    )(flag, *operands)


def down_kernel(flag, first, last, own, copied, near, across, brought, far, out_main, out_rest):
    home = flag[0] == 1
    panels = (
        (first[:, :QUARTER], jnp.where(home, own[...], copied[...])),
        (first[:, QUARTER : 2 * QUARTER], near[...]),
        (first[:, 2 * QUARTER : 3 * QUARTER], across[...]),
        (
            jnp.concatenate([first[:, 3 * QUARTER :], last[...]], axis=1),
            jnp.where(home, brought[...], far[...]),
        ),
    )
    total = None
    for hidden, weights in panels:
        term = jnp.dot(hidden, weights, preferred_element_type=jnp.float32)
        total = term if total is None else total + term
    total = total.astype(out_main.dtype)
    out_main[:, :8] = total[:MAIN].reshape(-1, 8, TILE)
    out_main[:, 8:] = total[MAIN : 2 * MAIN].reshape(-1, 8, TILE)
    out_rest[...] = total[2 * MAIN :]


def down_rows(flag, first, last, panels, step, starts):
    rows = 2 * MAIN + REST

    def panel(wanted, start):
        skip = start // TILE
        if wanted is None:
            return pl.BlockSpec((QUARTER, TILE), lambda i, f: (0, skip + i))
        return pl.BlockSpec((QUARTER, TILE), lambda i, f: (0, pick_block(f, wanted, skip + i)))

    main, tail = pl.pallas_call(
        down_kernel,
        grid_spec=pltpu.PrefetchScalarGridSpec(
            num_scalar_prefetch=1,
            grid=(step // TILE,),
            in_specs=[
                pl.BlockSpec(first.shape, lambda i, f: (0, 0)),
                pl.BlockSpec(last.shape, lambda i, f: (0, 0)),
                *map(panel, (1, 0, None, None, 1, 0), starts),
            ],
            out_specs=[
                pl.BlockSpec((MAIN // 8, 16, TILE), lambda i, f: (0, 0, i)),
                pl.BlockSpec((REST, TILE), lambda i, f: (0, i)),
            ],
        ),
        out_shape=[
            jax.ShapeDtypeStruct((MAIN // 8, 16, step), jnp.bfloat16),
            jax.ShapeDtypeStruct((REST, step), jnp.bfloat16),
        ],
        compiler_params=pltpu.CompilerParams(vmem_limit_bytes=32 * 2**20),
        cost_estimate=pl.CostEstimate(
            flops=8 * rows * QUARTER * step,
            bytes_accessed=2 * (4 * QUARTER * step + rows * (4 * QUARTER + step)),
            transcendentals=0,
        ),
    )(flag, first, last, *panels)
    return main.reshape(2 * MAIN, step), tail


def pair_exchange(value):
    return lax.ppermute(value, ("zh", "zl"), PAIR)


def body(tokens, route_ids, route_gates, gate_weight, up_weight, down_weight):
    tok_rows, width = tokens.shape
    chips = lax.axis_size("y") * lax.axis_size("x")
    side = lax.axis_index("zh")
    flag = (lax.axis_index("c") == side).astype(jnp.int32).reshape(1)

    routes = jnp.concatenate([route_ids.astype(jnp.float32), route_gates], axis=1)
    high = lax.reduce_precision(route_gates, 8, 7)
    extra = jnp.concatenate([route_ids.astype(jnp.float32), high, route_gates - high], axis=1)
    extra = jnp.pad(extra.astype(jnp.bfloat16), ((0, 0), (0, 128 - extra.shape[1])))
    other = pair_exchange(jnp.concatenate([tokens, extra], axis=1))

    top = route_ids.shape[1]
    hosted = (2 * jnp.arange(chips, dtype=jnp.int32) + side).astype(jnp.float32)
    place = jnp.arange(tok_rows)
    earlier = (place[:, None] > place[None, :]).astype(jnp.bfloat16)

    def slots(table, shift):
        match = (table[:, :top, None] == hosted[None, None, :]).astype(jnp.float32)
        named = jnp.sum(match, axis=1)
        weight = jnp.sum(table[:, top:, None] * match, axis=1)
        rank = jnp.dot(earlier, named.astype(jnp.bfloat16), preferred_element_type=jnp.float32)
        rank = jnp.where(named > 0, rank.astype(jnp.int32), -1)[:, :, None]
        on_tile = rank == jnp.arange(16)
        on_rest = (rank - 16 + 4 * shift == jnp.arange(8)) & (rank >= 16)
        on_main = jnp.zeros_like(on_tile[:, :, :8])
        halves = [on_tile[:, :, :8], on_tile[:, :, 8:]]
        on_main = jnp.concatenate(
            [piece for half in halves for piece in ((on_main, half) if shift else (half, on_main))],
            axis=2,
        )
        return (
            *(jnp.transpose(on, (1, 2, 0)).astype(jnp.bfloat16) for on in (on_tile, on_rest)),
            *(jnp.where(on, weight[:, :, None], 0.0) for on in (on_main, on_rest)),
        )

    def rows_of(part, rows):
        flat = part.reshape(-1, rows.shape[0])
        return jnp.dot(flat, rows, preferred_element_type=jnp.float32).astype(jnp.bfloat16)

    def exchange_main(rows):
        parts = rows.reshape(2 * chips, -1, rows.shape[1])
        return lax.all_to_all(parts, EXP, 0, 0, tiled=True).reshape(rows.shape)

    def exchange_rest(rows):
        parts = rows.reshape(chips, 8, rows.shape[1])
        return lax.all_to_all(parts, ("y", "x"), 0, 0, tiled=True).reshape(rows.shape)

    pick, pick_rest, mix_own, mix_own_rest = slots(routes, 0)
    sent = rows_of(pick, tokens)
    mine = exchange_main(sent)
    other = after(other, sent)
    extra, other = other[:, width:].astype(jnp.float32), other[:, :width]
    ids, gate, low = (extra[:, at : at + 8] for at in (0, 8, 16))
    other_routes = jnp.concatenate([ids, gate + low], axis=1)

    owns = [
        jnp.concatenate(
            [after(gate_weight[0], got)[at : at + HALF], up_weight[0][at : at + HALF]], axis=0
        )
        for at, got in ((0, other), (HALF, other))
    ]
    owns[0] = jnp.concatenate([owns[0], down_weight[0][:, : STEPS[0]]], axis=1)
    nears = [along(own, NEXT) for own in owns]

    pick, other_rest, mix_other, mix_other_rest = slots(other_routes, 1)
    rest = rows_of(
        jnp.concatenate([pick_rest, other_rest], axis=2), jnp.concatenate([tokens, other], axis=0)
    )
    theirs = exchange_main(after(rows_of(pick, other), mine))
    fars = [along(owns[0], FAR), along(after(owns[1], nears[0], theirs), FAR)]
    copied = [along(own, FROM_HOME) for own in owns]
    whole = down_weight[0], along(after(down_weight[0], *copied), FROM_HOME)
    across_0 = along(after(nears[0], theirs), SIBLING)
    brought_0 = along(after(fars[0], theirs), TO_HOME)
    rest = exchange_rest(after(rest, theirs, across_0, brought_0, whole[1]))
    across = [across_0, along(after(nears[1], rest), SIBLING)]

    def halves(*parts):
        part = jnp.concatenate([part.reshape(tok_rows, -1) for part in parts], axis=0)
        high = lax.reduce_precision(part, 8, 7)
        return jnp.concatenate([high, part - high], axis=0).astype(jnp.bfloat16)

    mix_main, mix_rest = halves(mix_own, mix_other), halves(mix_own_rest, mix_other_rest)
    count = 2 * tok_rows

    def columns(at, step, *earlier):
        own = after(down_weight[0][:, at : at + step], *earlier)
        return along(own, NEXT), along(own, FAR)

    units = [*zip(owns, copied, strict=True), *zip(nears), *zip(across), (brought_0, fars[0])]
    first = hidden_units(flag, after(mine, whole[1]), theirs, rest, units)
    brought_1 = along(after(fars[1], first), TO_HOME)
    down_1 = columns(STEPS[0], STEPS[1], fars[1], first)
    last = hidden_units(flag, after(mine, first), theirs, rest, [(brought_1, fars[1])])
    panels = owns[0], copied[0], nears[0], across[0], brought_0, fars[0]
    result_0 = down_rows(flag, first, last, panels, STEPS[0], (width,) * 6)
    at = STEPS[0] + STEPS[1]
    down_2 = columns(at, STEPS[2], down_1[1], result_0[0])
    panels = whole + share(*down_1, result_0[0])
    result_1 = down_rows(flag, first, last, panels, STEPS[1], (STEPS[0],) * 2 + (0,) * 4)
    panels = whole + share(*down_2, result_1[0])
    result_2 = down_rows(flag, first, last, panels, STEPS[2], (at,) * 2 + (0,) * 4)
    mains, rests = zip(result_0, result_1, result_2, strict=True)
    back_0 = exchange_main(mains[0])
    back_1 = exchange_main(after(mains[1], back_0))
    back_rest = exchange_rest(after(jnp.concatenate(rests, axis=1), back_1))
    back_2 = exchange_main(after(mains[2], back_rest))
    outs, at = [], 0
    for back in (back_0, back_1, back_2):
        tail = back_rest[:, at : at + back.shape[1]]
        at += back.shape[1]
        sums = jnp.dot(mix_main, back, preferred_element_type=jnp.float32) + jnp.dot(
            mix_rest, tail, preferred_element_type=jnp.float32
        )
        sums = sums[:count] + sums[count:]
        partner = pair_exchange(sums[tok_rows:].astype(jnp.bfloat16))
        outs.append((sums[:tok_rows] + partner.astype(jnp.float32)).astype(jnp.bfloat16))
    return jnp.concatenate(outs, axis=1)


def solution(mesh):
    fine = Mesh(mesh.devices.reshape(4, 4, 2, 2, 2), ALL)
    rows = P(ALL, None)
    panels = P(EXP, ("zh", "zl"), None)
    return jax.shard_map(
        body,
        mesh=fine,
        in_specs=(rows, rows, rows, panels, panels, panels),
        out_specs=rows,
        check_vma=False,
    )
```

```python
import functools

import jax
import jax.numpy as jnp
from jax import lax
from jax.experimental import pallas as pl
from jax.experimental.pallas import tpu as pltpu
from jax.sharding import Mesh, PartitionSpec as P

EXP = ("y", "x", "c")
COL = ("c", "zh", "zl")
ALL = ("y", "x", "c", "zh", "zl")


def swaps(*pairs):
    return [way for a, b in pairs for way in ((a, b), (b, a))]


PAIR = swaps((0, 3), (1, 2))
NEXT = swaps((0, 1), (6, 7), (4, 3), (5, 2))
FAR = swaps((5, 3), (4, 2))
SIBLING = swaps((0, 4), (1, 5), (2, 6), (3, 7))
FROM_HOME = [(0, 4), (1, 5), (6, 2), (7, 3)]
TO_HOME = [(b, a) for a, b in FROM_HOME]
STEPS = (1792, 2688, 2688)
QUARTER = 256
HALF = 128
MAIN = 256
REST = 128
TILE = 896
DEEP = 1792


def along(value, pairs):
    return lax.ppermute(value, COL, pairs)


def after(value, *earlier):
    return lax.optimization_barrier((value, *earlier))[0]


def share(near, far, earlier):
    across = along(after(near, earlier), SIBLING)
    brought = along(after(far, earlier), TO_HOME)
    return near, across, brought, far


def pick_block(flag, wanted, block):
    return jnp.where(flag[0] == wanted, block, 0)


def hidden_kernel(flag, mine, theirs, rest, *refs, kinds):
    panels, out, total = refs[:-2], refs[-2], refs[-1]
    part = pl.program_id(0)

    @pl.when(part == 0)
    def _():
        total[...] = jnp.zeros_like(total)

    at = 0
    for unit, kind in enumerate(kinds):
        panel = panels[at][...]
        if kind == 2:
            panel = jnp.where(flag[0] == 1, panel, panels[at + 1][...])
        for rows, first in ((mine, 0), (theirs, MAIN), (rest, 2 * MAIN)):
            total[pl.ds(first, rows.shape[0]), pl.ds(unit * 2 * HALF, 2 * HALF)] += lax.dot_general(
                rows[...], panel, (((1,), (1,)), ((), ())), preferred_element_type=jnp.float32
            )
        at += kind

    @pl.when(part == pl.num_programs(0) - 1)
    def _():
        for unit in range(len(kinds)):
            gate = total[:, pl.ds(unit * 2 * HALF, HALF)]
            upper = total[:, pl.ds(unit * 2 * HALF + HALF, HALF)]
            hidden = gate / (1.0 + jnp.exp(-gate)) * upper
            out[:, pl.ds(unit * HALF, HALF)] = hidden.astype(out.dtype)


def hidden_units(flag, mine, theirs, rest, units):
    rows, width = 2 * MAIN + REST, rest.shape[1]
    kinds = tuple(len(unit) for unit in units)
    specs = [pl.BlockSpec((part.shape[0], DEEP), lambda i, f: (0, i)) for part in (mine, theirs, rest)]
    operands = [mine, theirs, rest]
    for unit in units:
        for place, panel in enumerate(unit):
            if len(unit) == 1:
                spec = pl.BlockSpec((2 * HALF, DEEP), lambda i, f: (0, i))
            else:
                spec = pl.BlockSpec(
                    (2 * HALF, DEEP), lambda i, f, w=1 - place: (0, pick_block(f, w, i))
                )
            specs.append(spec)
            operands.append(panel)
    return pl.pallas_call(
        functools.partial(hidden_kernel, kinds=kinds),
        grid_spec=pltpu.PrefetchScalarGridSpec(
            num_scalar_prefetch=1,
            grid=(width // DEEP,),
            in_specs=specs,
            out_specs=pl.BlockSpec((rows, len(units) * HALF), lambda i, f: (0, 0)),
            scratch_shapes=[pltpu.VMEM((rows, len(units) * 2 * HALF), jnp.float32)],
        ),
        out_shape=jax.ShapeDtypeStruct((rows, len(units) * HALF), jnp.bfloat16),
        compiler_params=pltpu.CompilerParams(vmem_limit_bytes=48 * 2**20),
        cost_estimate=pl.CostEstimate(flops=1, bytes_accessed=1, transcendentals=0),
    )(flag, *operands)


def down_kernel(flag, first, last, own, copied, near, across, brought, far, out_main, out_rest):
    home = flag[0] == 1
    panels = (
        (first[:, :QUARTER], jnp.where(home, own[...], copied[...])),
        (first[:, QUARTER : 2 * QUARTER], near[...]),
        (first[:, 2 * QUARTER : 3 * QUARTER], across[...]),
        (
            jnp.concatenate([first[:, 3 * QUARTER :], last[...]], axis=1),
            jnp.where(home, brought[...], far[...]),
        ),
    )
    total = None
    for hidden, weights in panels:
        term = jnp.dot(hidden, weights, preferred_element_type=jnp.float32)
        total = term if total is None else total + term
    total = total.astype(out_main.dtype)
    out_main[:, :8] = total[:MAIN].reshape(-1, 8, TILE)
    out_main[:, 8:] = total[MAIN : 2 * MAIN].reshape(-1, 8, TILE)
    out_rest[...] = total[2 * MAIN :]


def down_rows(flag, first, last, panels, step, starts):
    rows = 2 * MAIN + REST

    def panel(wanted, start):
        skip = start // TILE
        if wanted is None:
            return pl.BlockSpec((QUARTER, TILE), lambda i, f: (0, skip + i))
        return pl.BlockSpec((QUARTER, TILE), lambda i, f: (0, pick_block(f, wanted, skip + i)))

    main, tail = pl.pallas_call(
        down_kernel,
        grid_spec=pltpu.PrefetchScalarGridSpec(
            num_scalar_prefetch=1,
            grid=(step // TILE,),
            in_specs=[
                pl.BlockSpec(first.shape, lambda i, f: (0, 0)),
                pl.BlockSpec(last.shape, lambda i, f: (0, 0)),
                *map(panel, (1, 0, None, None, 1, 0), starts),
            ],
            out_specs=[
                pl.BlockSpec((MAIN // 8, 16, TILE), lambda i, f: (0, 0, i)),
                pl.BlockSpec((REST, TILE), lambda i, f: (0, i)),
            ],
        ),
        out_shape=[
            jax.ShapeDtypeStruct((MAIN // 8, 16, step), jnp.bfloat16),
            jax.ShapeDtypeStruct((REST, step), jnp.bfloat16),
        ],
        compiler_params=pltpu.CompilerParams(vmem_limit_bytes=32 * 2**20),
        cost_estimate=pl.CostEstimate(
            flops=8 * rows * QUARTER * step,
            bytes_accessed=2 * (4 * QUARTER * step + rows * (4 * QUARTER + step)),
            transcendentals=0,
        ),
    )(flag, first, last, *panels)
    return main.reshape(2 * MAIN, step), tail


def pair_exchange(value):
    return lax.ppermute(value, ("zh", "zl"), PAIR)


def body(tokens, route_ids, route_gates, gate_weight, up_weight, down_weight):
    tok_rows, width = tokens.shape
    chips = lax.axis_size("y") * lax.axis_size("x")
    side = lax.axis_index("zh")
    flag = (lax.axis_index("c") == side).astype(jnp.int32).reshape(1)

    routes = jnp.concatenate([route_ids.astype(jnp.float32), route_gates], axis=1)
    high = lax.reduce_precision(route_gates, 8, 7)
    extra = jnp.concatenate([route_ids.astype(jnp.float32), high, route_gates - high], axis=1)
    extra = jnp.pad(extra.astype(jnp.bfloat16), ((0, 0), (0, 128 - extra.shape[1])))
    other = pair_exchange(jnp.concatenate([tokens, extra], axis=1))

    top = route_ids.shape[1]
    hosted = (2 * jnp.arange(chips, dtype=jnp.int32) + side).astype(jnp.float32)
    place = jnp.arange(tok_rows)
    earlier = (place[:, None] > place[None, :]).astype(jnp.bfloat16)

    def slots(table, shift):
        match = (table[:, :top, None] == hosted[None, None, :]).astype(jnp.float32)
        named = jnp.sum(match, axis=1)
        weight = jnp.sum(table[:, top:, None] * match, axis=1)
        rank = jnp.dot(earlier, named.astype(jnp.bfloat16), preferred_element_type=jnp.float32)
        rank = jnp.where(named > 0, rank.astype(jnp.int32), -1)[:, :, None]
        on_tile = rank == jnp.arange(16)
        on_rest = (rank - 16 + 4 * shift == jnp.arange(8)) & (rank >= 16)
        on_main = jnp.zeros_like(on_tile[:, :, :8])
        halves = [on_tile[:, :, :8], on_tile[:, :, 8:]]
        on_main = jnp.concatenate(
            [piece for half in halves for piece in ((on_main, half) if shift else (half, on_main))],
            axis=2,
        )
        return (
            *(jnp.transpose(on, (1, 2, 0)).astype(jnp.bfloat16) for on in (on_tile, on_rest)),
            *(jnp.where(on, weight[:, :, None], 0.0) for on in (on_main, on_rest)),
        )

    def rows_of(part, rows):
        flat = part.reshape(-1, rows.shape[0])
        return jnp.dot(flat, rows, preferred_element_type=jnp.float32).astype(jnp.bfloat16)

    def exchange_main(rows):
        parts = rows.reshape(2 * chips, -1, rows.shape[1])
        return lax.all_to_all(parts, EXP, 0, 0, tiled=True).reshape(rows.shape)

    def exchange_rest(rows):
        parts = rows.reshape(chips, 8, rows.shape[1])
        return lax.all_to_all(parts, ("y", "x"), 0, 0, tiled=True).reshape(rows.shape)

    pick, pick_rest, mix_own, mix_own_rest = slots(routes, 0)
    sent = rows_of(pick, tokens)
    mine = exchange_main(sent)
    other = after(other, sent)
    extra, other = other[:, width:].astype(jnp.float32), other[:, :width]
    ids, gate, low = (extra[:, at : at + 8] for at in (0, 8, 16))
    other_routes = jnp.concatenate([ids, gate + low], axis=1)

    owns = [
        jnp.concatenate(
            [after(gate_weight[0], got)[at : at + HALF], up_weight[0][at : at + HALF]], axis=0
        )
        for at, got in ((0, other), (HALF, other))
    ]
    owns[0] = jnp.concatenate([owns[0], down_weight[0][:, : STEPS[0]]], axis=1)
    nears = [along(own, NEXT) for own in owns]

    pick, other_rest, mix_other, mix_other_rest = slots(other_routes, 1)
    rest = rows_of(
        jnp.concatenate([pick_rest, other_rest], axis=2), jnp.concatenate([tokens, other], axis=0)
    )
    theirs = exchange_main(after(rows_of(pick, other), mine, nears[0]))
    copied = [along(own, FROM_HOME) for own in owns]
    whole = down_weight[0], along(after(down_weight[0], copied[0]), FROM_HOME)
    rest = exchange_rest(after(rest, theirs, whole[1], copied[1]))
    fars = [along(owns[0], FAR), along(after(owns[1], nears[0], theirs), FAR)]
    across = [
        along(after(near, got), SIBLING) for near, got in zip(nears, (theirs, rest), strict=True)
    ]
    brought_0 = along(after(fars[0], rest), TO_HOME)

    def halves(*parts):
        part = jnp.concatenate([part.reshape(tok_rows, -1) for part in parts], axis=0)
        high = lax.reduce_precision(part, 8, 7)
        return jnp.concatenate([high, part - high], axis=0).astype(jnp.bfloat16)

    mix_main, mix_rest = halves(mix_own, mix_other), halves(mix_own_rest, mix_other_rest)
    count = 2 * tok_rows

    def columns(at, step, *earlier):
        own = after(down_weight[0][:, at : at + step], *earlier)
        return along(own, NEXT), along(own, FAR)

    units = [*zip(owns, copied, strict=True), *zip(nears), *zip(across), (brought_0, fars[0])]
    first = hidden_units(flag, after(mine, whole[1]), theirs, rest, units)
    brought_1 = along(after(fars[1], first), TO_HOME)
    down_1 = columns(STEPS[0], STEPS[1], fars[1], first)
    last = hidden_units(flag, after(mine, first), theirs, rest, [(brought_1, fars[1])])
    panels = owns[0], copied[0], nears[0], across[0], brought_0, fars[0]
    result_0 = down_rows(flag, first, last, panels, STEPS[0], (width,) * 6)
    at = STEPS[0] + STEPS[1]
    down_2 = columns(at, STEPS[2], down_1[1], result_0[0])
    panels = whole + share(*down_1, result_0[0])
    result_1 = down_rows(flag, first, last, panels, STEPS[1], (STEPS[0],) * 2 + (0,) * 4)
    panels = whole + share(*down_2, result_1[0])
    result_2 = down_rows(flag, first, last, panels, STEPS[2], (at,) * 2 + (0,) * 4)
    mains, rests = zip(result_0, result_1, result_2, strict=True)
    back_0 = exchange_main(mains[0])
    back_1 = exchange_main(after(mains[1], back_0))
    back_rest = exchange_rest(after(jnp.concatenate(rests, axis=1), back_1))
    back_2 = exchange_main(after(mains[2], back_rest))
    outs, at = [], 0
    for back in (back_0, back_1, back_2):
        tail = back_rest[:, at : at + back.shape[1]]
        at += back.shape[1]
        sums = jnp.dot(mix_main, back, preferred_element_type=jnp.float32) + jnp.dot(
            mix_rest, tail, preferred_element_type=jnp.float32
        )
        sums = sums[:count] + sums[count:]
        partner = pair_exchange(sums[tok_rows:].astype(jnp.bfloat16))
        outs.append((sums[:tok_rows] + partner.astype(jnp.float32)).astype(jnp.bfloat16))
    return jnp.concatenate(outs, axis=1)


def solution(mesh):
    fine = Mesh(mesh.devices.reshape(4, 4, 2, 2, 2), ALL)
    rows = P(ALL, None)
    panels = P(EXP, ("zh", "zl"), None)
    return jax.shard_map(
        body,
        mesh=fine,
        in_specs=(rows, rows, rows, panels, panels, panels),
        out_specs=rows,
        check_vma=False,
    )
```

```python
import functools

import jax
import jax.numpy as jnp
from jax import lax
from jax.experimental import pallas as pl
from jax.experimental.pallas import tpu as pltpu
from jax.sharding import Mesh, PartitionSpec as P

EXP = ("y", "x", "c")
COL = ("c", "zh", "zl")
ALL = ("y", "x", "c", "zh", "zl")


def swaps(*pairs):
    return [way for a, b in pairs for way in ((a, b), (b, a))]


PAIR = swaps((0, 3), (1, 2))
NEXT = swaps((0, 1), (6, 7), (4, 3), (5, 2))
FAR = swaps((5, 3), (4, 2))
SIBLING = swaps((0, 4), (1, 5), (2, 6), (3, 7))
FROM_HOME = [(0, 4), (1, 5), (6, 2), (7, 3)]
TO_HOME = [(b, a) for a, b in FROM_HOME]
STEPS = (1792, 2688, 2688)
QUARTER = 256
HALF = 128
MAIN = 256
REST = 128
TILE = 896
DEEP = 1792


def along(value, pairs):
    return lax.ppermute(value, COL, pairs)


def after(value, *earlier):
    return lax.optimization_barrier((value, *earlier))[0]


def share(near, far, earlier):
    across = along(after(near, earlier), SIBLING)
    brought = along(after(far, earlier), TO_HOME)
    return near, across, brought, far


def pick_block(flag, wanted, block):
    return jnp.where(flag[0] == wanted, block, 0)


def hidden_kernel(flag, mine, theirs, rest, *refs, kinds):
    panels, out, total = refs[:-2], refs[-2], refs[-1]
    part = pl.program_id(0)

    @pl.when(part == 0)
    def _():
        total[...] = jnp.zeros_like(total)

    at = 0
    for unit, kind in enumerate(kinds):
        panel = panels[at][...]
        if kind == 2:
            panel = jnp.where(flag[0] == 1, panel, panels[at + 1][...])
        for rows, first in ((mine, 0), (theirs, MAIN), (rest, 2 * MAIN)):
            total[pl.ds(first, rows.shape[0]), pl.ds(unit * 2 * HALF, 2 * HALF)] += lax.dot_general(
                rows[...], panel, (((1,), (1,)), ((), ())), preferred_element_type=jnp.float32
            )
        at += kind

    @pl.when(part == pl.num_programs(0) - 1)
    def _():
        for unit in range(len(kinds)):
            gate = total[:, pl.ds(unit * 2 * HALF, HALF)]
            upper = total[:, pl.ds(unit * 2 * HALF + HALF, HALF)]
            hidden = gate / (1.0 + jnp.exp(-gate)) * upper
            out[:, pl.ds(unit * HALF, HALF)] = hidden.astype(out.dtype)


def hidden_units(flag, mine, theirs, rest, units):
    rows, width = 2 * MAIN + REST, rest.shape[1]
    kinds = tuple(len(unit) for unit in units)
    specs = [pl.BlockSpec((part.shape[0], DEEP), lambda i, f: (0, i)) for part in (mine, theirs, rest)]
    operands = [mine, theirs, rest]
    for unit in units:
        for place, panel in enumerate(unit):
            if len(unit) == 1:
                spec = pl.BlockSpec((2 * HALF, DEEP), lambda i, f: (0, i))
            else:
                spec = pl.BlockSpec(
                    (2 * HALF, DEEP), lambda i, f, w=1 - place: (0, pick_block(f, w, i))
                )
            specs.append(spec)
            operands.append(panel)
    return pl.pallas_call(
        functools.partial(hidden_kernel, kinds=kinds),
        grid_spec=pltpu.PrefetchScalarGridSpec(
            num_scalar_prefetch=1,
            grid=(width // DEEP,),
            in_specs=specs,
            out_specs=pl.BlockSpec((rows, len(units) * HALF), lambda i, f: (0, 0)),
            scratch_shapes=[pltpu.VMEM((rows, len(units) * 2 * HALF), jnp.float32)],
        ),
        out_shape=jax.ShapeDtypeStruct((rows, len(units) * HALF), jnp.bfloat16),
        compiler_params=pltpu.CompilerParams(vmem_limit_bytes=48 * 2**20),
        cost_estimate=pl.CostEstimate(flops=1, bytes_accessed=1, transcendentals=0),
    )(flag, *operands)


def down_kernel(flag, first, last, own, copied, near, across, brought, far, out_main, out_rest):
    home = flag[0] == 1
    panels = (
        (first[:, :QUARTER], jnp.where(home, own[...], copied[...])),
        (first[:, QUARTER : 2 * QUARTER], near[...]),
        (first[:, 2 * QUARTER : 3 * QUARTER], across[...]),
        (
            jnp.concatenate([first[:, 3 * QUARTER :], last[...]], axis=1),
            jnp.where(home, brought[...], far[...]),
        ),
    )
    total = None
    for hidden, weights in panels:
        term = jnp.dot(hidden, weights, preferred_element_type=jnp.float32)
        total = term if total is None else total + term
    total = total.astype(out_main.dtype)
    out_main[:, :8] = total[:MAIN].reshape(-1, 8, TILE)
    out_main[:, 8:] = total[MAIN : 2 * MAIN].reshape(-1, 8, TILE)
    out_rest[...] = total[2 * MAIN :]


def down_rows(flag, first, last, panels, step, starts):
    rows = 2 * MAIN + REST

    def panel(wanted, start):
        skip = start // TILE
        if wanted is None:
            return pl.BlockSpec((QUARTER, TILE), lambda i, f: (0, skip + i))
        return pl.BlockSpec((QUARTER, TILE), lambda i, f: (0, pick_block(f, wanted, skip + i)))

    main, tail = pl.pallas_call(
        down_kernel,
        grid_spec=pltpu.PrefetchScalarGridSpec(
            num_scalar_prefetch=1,
            grid=(step // TILE,),
            in_specs=[
                pl.BlockSpec(first.shape, lambda i, f: (0, 0)),
                pl.BlockSpec(last.shape, lambda i, f: (0, 0)),
                *map(panel, (1, 0, None, None, 1, 0), starts),
            ],
            out_specs=[
                pl.BlockSpec((MAIN // 8, 16, TILE), lambda i, f: (0, 0, i)),
                pl.BlockSpec((REST, TILE), lambda i, f: (0, i)),
            ],
        ),
        out_shape=[
            jax.ShapeDtypeStruct((MAIN // 8, 16, step), jnp.bfloat16),
            jax.ShapeDtypeStruct((REST, step), jnp.bfloat16),
        ],
        compiler_params=pltpu.CompilerParams(vmem_limit_bytes=32 * 2**20),
        cost_estimate=pl.CostEstimate(
            flops=8 * rows * QUARTER * step,
            bytes_accessed=2 * (4 * QUARTER * step + rows * (4 * QUARTER + step)),
            transcendentals=0,
        ),
    )(flag, first, last, *panels)
    return main.reshape(2 * MAIN, step), tail


def pair_exchange(value):
    return lax.ppermute(value, ("zh", "zl"), PAIR)


def body(tokens, route_ids, route_gates, gate_weight, up_weight, down_weight):
    tok_rows, width = tokens.shape
    chips = lax.axis_size("y") * lax.axis_size("x")
    side = lax.axis_index("zh")
    flag = (lax.axis_index("c") == side).astype(jnp.int32).reshape(1)

    routes = jnp.concatenate([route_ids.astype(jnp.float32), route_gates], axis=1)
    high = lax.reduce_precision(route_gates, 8, 7)
    extra = jnp.concatenate([route_ids.astype(jnp.float32), high, route_gates - high], axis=1)
    extra = jnp.pad(extra.astype(jnp.bfloat16), ((0, 0), (0, 128 - extra.shape[1])))
    other = pair_exchange(jnp.concatenate([tokens, extra], axis=1))

    top = route_ids.shape[1]
    hosted = (2 * jnp.arange(chips, dtype=jnp.int32) + side).astype(jnp.float32)
    place = jnp.arange(tok_rows)
    earlier = (place[:, None] > place[None, :]).astype(jnp.bfloat16)

    def slots(table, shift):
        match = (table[:, :top, None] == hosted[None, None, :]).astype(jnp.float32)
        named = jnp.sum(match, axis=1)
        weight = jnp.sum(table[:, top:, None] * match, axis=1)
        rank = jnp.dot(earlier, named.astype(jnp.bfloat16), preferred_element_type=jnp.float32)
        rank = jnp.where(named > 0, rank.astype(jnp.int32), -1)[:, :, None]
        on_tile = rank == jnp.arange(16)
        on_rest = (rank - 16 + 4 * shift == jnp.arange(8)) & (rank >= 16)
        on_main = jnp.zeros_like(on_tile[:, :, :8])
        halves = [on_tile[:, :, :8], on_tile[:, :, 8:]]
        on_main = jnp.concatenate(
            [piece for half in halves for piece in ((on_main, half) if shift else (half, on_main))],
            axis=2,
        )
        return (
            *(jnp.transpose(on, (1, 2, 0)).astype(jnp.bfloat16) for on in (on_tile, on_rest)),
            *(jnp.where(on, weight[:, :, None], 0.0) for on in (on_main, on_rest)),
        )

    def rows_of(part, rows):
        flat = part.reshape(-1, rows.shape[0])
        return jnp.dot(flat, rows, preferred_element_type=jnp.float32).astype(jnp.bfloat16)

    def exchange_main(rows):
        parts = rows.reshape(2 * chips, -1, rows.shape[1])
        return lax.all_to_all(parts, EXP, 0, 0, tiled=True).reshape(rows.shape)

    def exchange_rest(rows):
        parts = rows.reshape(chips, 8, rows.shape[1])
        return lax.all_to_all(parts, ("y", "x"), 0, 0, tiled=True).reshape(rows.shape)

    pick, pick_rest, mix_own, mix_own_rest = slots(routes, 0)
    sent = rows_of(pick, tokens)
    mine = exchange_main(sent)
    other = after(other, sent)
    extra, other = other[:, width:].astype(jnp.float32), other[:, :width]
    ids, gate, low = (extra[:, at : at + 8] for at in (0, 8, 16))
    other_routes = jnp.concatenate([ids, gate + low], axis=1)

    owns = [
        jnp.concatenate(
            [after(gate_weight[0], got)[at : at + HALF], up_weight[0][at : at + HALF]], axis=0
        )
        for at, got in ((0, sent), (HALF, other))
    ]
    owns[0] = jnp.concatenate([owns[0], down_weight[0][:, : STEPS[0]]], axis=1)
    owns[0] = after(owns[0], other)
    nears = [along(own, NEXT) for own in owns]

    pick, other_rest, mix_other, mix_other_rest = slots(other_routes, 1)
    rest = rows_of(
        jnp.concatenate([pick_rest, other_rest], axis=2), jnp.concatenate([tokens, other], axis=0)
    )
    theirs = exchange_main(after(rows_of(pick, other), mine, nears[0]))
    copied = [along(own, FROM_HOME) for own in owns]
    whole = down_weight[0], along(after(down_weight[0], copied[0]), FROM_HOME)
    rest = exchange_rest(after(rest, theirs, whole[1], copied[1]))
    fars = [along(owns[0], FAR), along(after(owns[1], nears[0], theirs), FAR)]
    across = [
        along(after(near, got), SIBLING) for near, got in zip(nears, (theirs, rest), strict=True)
    ]
    brought_0 = along(after(fars[0], rest), TO_HOME)

    def halves(*parts):
        part = jnp.concatenate([part.reshape(tok_rows, -1) for part in parts], axis=0)
        high = lax.reduce_precision(part, 8, 7)
        return jnp.concatenate([high, part - high], axis=0).astype(jnp.bfloat16)

    mix_main, mix_rest = halves(mix_own, mix_other), halves(mix_own_rest, mix_other_rest)
    count = 2 * tok_rows

    def columns(at, step, *earlier):
        own = after(down_weight[0][:, at : at + step], *earlier)
        return along(own, NEXT), along(own, FAR)

    units = [*zip(owns, copied, strict=True), *zip(nears), *zip(across), (brought_0, fars[0])]
    first = hidden_units(flag, after(mine, whole[1]), theirs, rest, units)
    brought_1 = along(after(fars[1], first), TO_HOME)
    down_1 = columns(STEPS[0], STEPS[1], fars[1], first)
    last = hidden_units(flag, after(mine, first), theirs, rest, [(brought_1, fars[1])])
    panels = owns[0], copied[0], nears[0], across[0], brought_0, fars[0]
    result_0 = down_rows(flag, first, last, panels, STEPS[0], (width,) * 6)
    at = STEPS[0] + STEPS[1]
    down_2 = columns(at, STEPS[2], down_1[1], result_0[0])
    panels = whole + share(*down_1, result_0[0])
    result_1 = down_rows(flag, first, last, panels, STEPS[1], (STEPS[0],) * 2 + (0,) * 4)
    panels = whole + share(*down_2, result_1[0])
    result_2 = down_rows(flag, first, last, panels, STEPS[2], (at,) * 2 + (0,) * 4)
    mains, rests = zip(result_0, result_1, result_2, strict=True)
    back_0 = exchange_main(mains[0])
    back_1 = exchange_main(after(mains[1], back_0))
    back_rest = exchange_rest(after(jnp.concatenate(rests, axis=1), back_1))
    back_2 = exchange_main(after(mains[2], back_rest))
    outs, at = [], 0
    for back in (back_0, back_1, back_2):
        tail = back_rest[:, at : at + back.shape[1]]
        at += back.shape[1]
        sums = jnp.dot(mix_main, back, preferred_element_type=jnp.float32) + jnp.dot(
            mix_rest, tail, preferred_element_type=jnp.float32
        )
        sums = sums[:count] + sums[count:]
        partner = pair_exchange(sums[tok_rows:].astype(jnp.bfloat16))
        outs.append((sums[:tok_rows] + partner.astype(jnp.float32)).astype(jnp.bfloat16))
    return jnp.concatenate(outs, axis=1)


def solution(mesh):
    fine = Mesh(mesh.devices.reshape(4, 4, 2, 2, 2), ALL)
    rows = P(ALL, None)
    panels = P(EXP, ("zh", "zl"), None)
    return jax.shard_map(
        body,
        mesh=fine,
        in_specs=(rows, rows, rows, panels, panels, panels),
        out_specs=rows,
        check_vma=False,
    )
```
